32 devices in a mesh: section: 4 (over y, core), expert: 8 (over z, x).
Axes of the slice: x: 2, y: 2, z: 4, core: 2. Of those that a mesh axis runs over, the one named last changes fastest.
Arguments:
- saved_inputs: bfloat16 [4, 2, 64, 2048], P('section', None, 'expert'), may hold values from -6 to 6
- top_grad: bfloat16 [2, 64, 2048], P(None, 'expert'), may hold values from -6 to 6
- expert_ids: int32 [4, 2, 64, 2], P('section', None, 'expert'), may hold values from 0 to 7, all different within a row; in each aligned block of 8 rows (0 to 7, 8 to 15, ..., all dimensions but the last counted through in order) at most 3 rows name the same one
- route_weights: bfloat16 [4, 2, 64, 2], P('section', None, 'expert'), may hold values from 0.099609375 to 0.59765625
- example_ids: int32 [2, 64], P(None, 'expert'), may hold values from 0 to 3, never falling along the last dimension, each value on 1 to 32 neighbouring positions
- gate_weight: bfloat16 [4, 12288, 2048], P('section', 'expert'), may hold values from -0.125 to 0.125
- up_weight: bfloat16 [4, 12288, 2048], P('section', 'expert'), may hold values from -0.125 to 0.125
- down_weight: bfloat16 [4, 12288, 2048], P('section', 'expert'), may hold values from -0.15625 to 0.15625
- left_proj: bfloat16 [4, 12288, 64], P('section', 'expert'), may hold values from -0.15625 to 0.15625
- right_proj: bfloat16 [4, 2048, 64], P('section'), may hold values from -0.125 to 0.125
Outputs:
- input_grads: bfloat16 [4, 2, 64, 2048], P('section', None, 'expert')
- sketches: float32 [4, 64, 4096], P('section', 'expert')
The draws below stay inside these ranges and needn't reach their ends.
Inputs may be any that keep to these rules, and one draw needn't show every extreme that they name: `expert_ids`: each row names 2 different experts; in each aligned block of 8 rows (one device's tokens of one layer and micro-batch) no expert is named by more than 3 rows, and some block reaches 3. `example_ids`: along each micro-batch the example number never falls and every example has a token.
All inputs are finite; a program needn't handle non-finite values.
Results may differ from the reference program's by a relative error of at most 0.028.
Values may be sent and summed in bfloat16 or wider, within the bound.
No kernel may reach another device: no remote copies, remote signals or barrier semaphores. Data moves between devices by JAX's collectives and lax.ppermute only.
A program may use at most 64 MiB of HBM per device.

```python
import math
import jax
import jax.numpy as jnp
import numpy as np
from jax import lax

D = 2048
FF = 1536
EXPERTS = 8
TOPK = 2
R = 64
MICRO = 2
EXM = 4
TOK_DEV = 8
CAP = 3
LAYERS = 4
TOKENS = 64
N_EXPERT = 8


def shard_levels(key, dims, cuts, least, high):
    def one(axis_at, shards_of):
        steps = jax.random.uniform(jax.random.fold_in(jax.random.fold_in(key, 6), axis_at), (shards_of,), jnp.float32, least / len(cuts), high / len(cuts))
        return jnp.repeat(jnp.exp(steps), dims[axis_at] // shards_of).reshape((-1,) + (1,) * (len(dims) - axis_at - 1))

    loudness = one(*cuts[0])
    for cut in cuts[1:]:
        loudness = loudness * one(*cut)
    return loudness


def length_profile(amount, total, limit, lean):
    weights = [(1 << 20) // math.isqrt(grade ** lean) + 1 for grade in range(2, amount + 1)]
    spare, counts = total - limit - (amount - 1), [1] * (amount - 1)
    while spare > 0:
        free = [i for i in range(amount - 1) if counts[i] < limit]
        whole, remaining = sum([weights[i] for i in free]), spare
        for i in free:
            extra = min(limit - counts[i], max(1, remaining * weights[i] // whole), spare)
            counts[i] = counts[i] + extra
            spare = spare - extra
    return np.array([limit] + counts)


def ragged_sizes(rng, amount, total, limit, skew):
    if amount == 2:
        one = jax.random.randint(rng, (), max(1, total - limit), min(limit, total - 1) + 1)
        return jnp.stack([one, total - one])
    tallies = jnp.asarray(length_profile(amount, total, limit, skew), jnp.int32)
    pairs = (amount - 1) // 2
    donor, taker = tallies[1:1 + 2 * pairs:2], tallies[2:2 + 2 * pairs:2]
    slack = jnp.minimum(donor - 1, limit - taker)
    shifted = jax.random.randint(jax.random.fold_in(rng, 1), (pairs,), 0, 1 << 20) % (slack + 1)
    tallies = tallies.at[1:1 + 2 * pairs:2].set(donor - shifted).at[2:2 + 2 * pairs:2].set(taker + shifted)
    return tallies[jax.random.permutation(jax.random.fold_in(rng, 2), amount)]


def shared_out(rng, own, number, rows, count, top, limit, lean):
    ranking = jax.random.permutation(rng, count)
    heavy_load, common = shares(count, rows * top, limit, lean, True), shares(count, rows * top, limit, lean, False)
    places = jnp.arange(count)

    def named(sizes, turn):
        used = int((sizes > 0).sum())
        fixed = max(1, used // 4)
        shifted = fixed + (places - fixed + turn * (used - fixed)) % max(1, count - fixed)
        return jnp.zeros((count,), jnp.int32).at[ranking[jnp.where(places < fixed, places, shifted)]].set(jnp.asarray(sizes, jnp.int32))

    sizes = jnp.where(number % 4 == 0, named(heavy_load, number // 4), named(common, number - number // 4 - 1))
    mixed = jax.random.permutation(jax.random.fold_in(own, 3), count)
    giver, receiver = mixed[0:count // 2 * 2:2], mixed[1:count // 2 * 2:2]
    slack = jnp.minimum(sizes[giver] - 1, limit - sizes[receiver]) // 2
    slack = jnp.where((giver == ranking[0]) | (receiver == ranking[0]) | (sizes[receiver] == 0), 0, jnp.maximum(slack, 0))
    shifted = jax.random.randint(jax.random.fold_in(own, 4), (count // 2,), 0, 1 << 20) % (slack + 1)
    sizes = sizes.at[giver].add(-shifted).at[receiver].add(shifted)
    members = jnp.searchsorted(jnp.cumsum(sizes), jnp.arange(rows * top), side="right").astype(jnp.int32)
    table = members.reshape(top, rows).T
    table = table[jax.random.permutation(jax.random.fold_in(own, 1), rows)]
    turn = jax.random.randint(jax.random.fold_in(own, 2), (rows, 1), 0, top)
    return jnp.take_along_axis(table, (jnp.arange(top)[None, :] + turn) % top, axis=1)


def shares(number_of, total, limit, lean, full):
    weights = [(1 << 20) // math.isqrt(standing ** lean) + 1 for standing in range(1, number_of + 1)]
    largest = limit if full else min(limit, max(-(-total // number_of), total * weights[0] // sum(weights)))
    least = 1 if total - largest >= number_of - 1 else 0
    counts, surplus = [largest] + [least] * (number_of - 1), total - largest - least * (number_of - 1)
    while surplus > 0:
        free = [i for i in range(1, number_of) if counts[i] < largest] or [i for i in range(1, number_of) if counts[i] < limit]
        pool, left = sum([weights[i] for i in free]), surplus
        for i in free:
            addition = min(limit - counts[i], max(1, left * weights[i] // pool), surplus)
            counts[i] = counts[i] + addition
            surplus = surplus - addition
    return np.array(counts)


def scatter_about(own_key, dims, scale, bound, split=(), kind=jnp.bfloat16):
    entries = scale * jax.random.normal(own_key, dims, jnp.float32)
    if split:
        entries = entries * shard_levels(own_key, dims, split, -0.22, 0.18)
    return jnp.clip(entries, -bound, bound).astype(kind)


def setup_inputs(seed: int = 0) -> dict:
    splits = jax.random.split(jax.random.key(seed), 11)
    saved_inputs = scatter_about(splits[0], (LAYERS, MICRO, TOKENS, D), 1.0, 6.0, ((0, 4), (2, 8)))
    top_grad = scatter_about(splits[1], (MICRO, TOKENS, D), 1.0, 6.0, ((1, 8),))
    expert_ids_keys = jax.random.split(jax.random.fold_in(splits[2], 1), LAYERS * MICRO * TOKENS // TOK_DEV)
    expert_ids_turns = jax.random.permutation(jax.random.fold_in(splits[2], 3), LAYERS * MICRO * TOKENS // TOK_DEV)
    expert_ids = jax.vmap(lambda own, number: shared_out(jax.random.fold_in(splits[2], 2), own, number, TOK_DEV, EXPERTS, TOPK, CAP, 2))(expert_ids_keys, expert_ids_turns).reshape((LAYERS, MICRO, TOKENS, TOPK))
    route_weights = jnp.clip(0.099609375 + 0.49804688 * jax.random.uniform(splits[3], (LAYERS, MICRO, TOKENS, TOPK), jnp.float32) ** shard_levels(splits[3], (LAYERS, MICRO, TOKENS, TOPK), ((0, 4), (2, 8)), -0.2, 0.2), 0.099609375, 0.59765625).astype(jnp.bfloat16)
    example_ids = jax.vmap(lambda own: jnp.searchsorted(jnp.cumsum(ragged_sizes(own, EXM, TOKENS, TOKENS // 2, 1)), jnp.arange(TOKENS), side="right"))(jax.random.split(splits[4], MICRO)).reshape((MICRO, TOKENS)).astype(jnp.int32)
    gate_weight = scatter_about(splits[5], (LAYERS, EXPERTS * FF, D), D ** -0.5, 0.125, ((0, 4), (1, 8)))
    up_weight = scatter_about(splits[6], (LAYERS, EXPERTS * FF, D), D ** -0.5, 0.125, ((0, 4), (1, 8)))
    down_weight = scatter_about(splits[7], (LAYERS, EXPERTS * FF, D), FF ** -0.5, 0.15625, ((0, 4), (1, 8)))
    left_proj = scatter_about(splits[8], (LAYERS, EXPERTS * FF, R), FF ** -0.5, 0.15625, ((0, 4), (1, 8)))
    right_proj = scatter_about(splits[9], (LAYERS, D, R), D ** -0.5, 0.125, ((0, 4),))
    return dict(saved_inputs=saved_inputs, top_grad=top_grad, expert_ids=expert_ids, route_weights=route_weights, example_ids=example_ids, gate_weight=gate_weight, up_weight=up_weight, down_weight=down_weight, left_proj=left_proj, right_proj=right_proj)


def reference(saved_inputs, top_grad, expert_ids, route_weights, example_ids, gate_weight, up_weight, down_weight, left_proj, right_proj):
    hsplit = N_EXPERT // EXPERTS
    group = FF // hsplit
    q_total = MICRO * EXM * EXPERTS

    def one_layer(out_grads, packed):
        inputs, route_ids, route_w, w_gate, w_up, w_down, proj_left, proj_right = packed
        w_gate = w_gate.reshape(EXPERTS, FF, D)
        w_up = w_up.reshape(EXPERTS, FF, D)
        w_down = w_down.reshape(EXPERTS, FF, D)
        proj_left = proj_left.reshape(EXPERTS, FF, R)
        new_list = []
        sketch = jnp.zeros((q_total * R, R), jnp.float32)
        for m in range(MICRO):
            acts = inputs[m]
            out_grad = out_grads[m]
            summed_grad = out_grad.astype(jnp.float32)
            right_tok = jnp.dot(out_grad, proj_right, preferred_element_type=jnp.float32)
            for e in range(EXPERTS):
                route = jnp.sum(jnp.where(route_ids[m] == e, route_w[m].astype(jnp.float32), jnp.float32(0.0)), axis=1)
                pre_gate = jnp.dot(acts, w_gate[e].T, preferred_element_type=jnp.float32)
                pre_up = jnp.dot(acts, w_up[e].T, preferred_element_type=jnp.float32)
                sigmoid_g = jax.nn.sigmoid(pre_gate)
                hidden = (pre_gate * sigmoid_g * pre_up).astype(jnp.bfloat16)
                left_part = jnp.einsum("tjh,jhr->tjr", hidden.reshape(TOKENS, hsplit, group).astype(jnp.float32),
                                       proj_left[e].reshape(hsplit, group, R).astype(jnp.float32))
                left_part = lax.optimization_barrier(left_part.astype(jnp.bfloat16))
                left_factor = jnp.sum(left_part.astype(jnp.float32), axis=1)
                grad_hidden = jnp.dot(out_grad, w_down[e].T, preferred_element_type=jnp.float32) * route[:, None]
                grad_gate = (grad_hidden * pre_up * sigmoid_g * (1.0 + pre_gate * (1.0 - sigmoid_g))).astype(jnp.bfloat16)
                grad_up = (grad_hidden * pre_gate * sigmoid_g).astype(jnp.bfloat16)
                part_grad = jnp.einsum("tjh,jhd->tjd", grad_gate.reshape(TOKENS, hsplit, group).astype(jnp.float32),
                                       w_gate[e].reshape(hsplit, group, D).astype(jnp.float32))
                part_grad = part_grad + jnp.einsum("tjh,jhd->tjd", grad_up.reshape(TOKENS, hsplit, group).astype(jnp.float32),
                                                   w_up[e].reshape(hsplit, group, D).astype(jnp.float32))
                part_grad = lax.optimization_barrier(part_grad.astype(jnp.bfloat16))
                summed_grad = summed_grad + jnp.sum(part_grad.astype(jnp.float32), axis=1)
                right_factor = right_tok * route[:, None]
                query = (m * EXM + example_ids[m]) * EXPERTS + e
                query_hot = (query[:, None] == jnp.arange(q_total, dtype=jnp.int32)[None, :]).astype(jnp.float32)
                outer_rows = (query_hot[:, :, None] * left_factor[:, None, :]).reshape(TOKENS, q_total * R)
                sketch = sketch + jnp.dot(outer_rows.T, right_factor, precision=lax.Precision.HIGHEST)
            new_list.append(summed_grad.astype(jnp.bfloat16))
        new_grads = jnp.stack(new_list)
        return new_grads, (new_grads, sketch.reshape(q_total, R * R))

    packed_all = (saved_inputs, expert_ids, route_weights, gate_weight, up_weight, down_weight, left_proj, right_proj)
    final_grads, outputs = lax.scan(one_layer, top_grad, packed_all, reverse=True)
    return outputs[0], outputs[1]
```

```python
import functools

import jax
import jax.numpy as jnp
from jax import lax
from jax.experimental import pallas as pl
from jax.experimental.pallas import tpu as pltpu
from jax.sharding import PartitionSpec as P

EXPERTS = 8
EXM = 4
CAP = 3
META = 128

F32 = jnp.float32
BF16 = jnp.bfloat16


def contract(a, b, dim_a, dim_b):
    return lax.dot_general(a, b, (((dim_a,), (dim_b,)), ((), ())), preferred_element_type=F32)


def iota(shape, dim):
    return lax.broadcasted_iota(jnp.int32, shape, dim)


def slots_of(ids, n_micro, tok_dev, n_expert, block):
    tokens = n_micro * tok_dev
    lanes = n_expert * block
    hsplit = n_expert // EXPERTS
    group = iota((tokens, lanes), 1) // (block * hsplit)
    hit = ids[:, 0:1] == group
    for k in range(1, ids.shape[1]):
        hit = hit | (ids[:, k : k + 1] == group)
    row, col = iota((tokens, tokens), 0), iota((tokens, tokens), 1)
    earlier = ((row // tok_dev == col // tok_dev) & (col < row)).astype(F32)
    position = contract(earlier, hit.astype(F32), 1, 0)
    slot = iota((tokens, lanes), 1) % block - (iota((tokens, lanes), 0) // tok_dev) * CAP
    return hit & (slot >= 0) & (slot < CAP) & (position.astype(jnp.int32) == slot), group


def prepare(n_expert, block, ids_ref, w_ref, ex_ref, x_ref, top_ref, send_ref, sel_ref, comb_ref):
    n_micro, tok_dev = x_ref.shape[1], x_ref.shape[2]
    tokens = n_micro * tok_dev
    feat = x_ref.shape[3]
    ids = jnp.concatenate([ids_ref[0, m] for m in range(n_micro)], axis=0)
    weights = jnp.concatenate([w_ref[0, m].astype(F32) for m in range(n_micro)], axis=0)
    mask, group = slots_of(ids, n_micro, tok_dev, n_expert, block)
    weight = jnp.where(ids[:, 0:1] == group, weights[:, 0:1], 0.0)
    for k in range(1, ids.shape[1]):
        weight = weight + jnp.where(ids[:, k : k + 1] == group, weights[:, k : k + 1], 0.0)
    comb = jnp.where(mask, weight, 0.0)
    sel_ref[...] = mask.astype(BF16)
    comb_ref[...] = comb.astype(BF16)
    twice = n_expert * 2 * block
    wide, _ = slots_of(ids, n_micro, tok_dev, n_expert, 2 * block)
    lane = iota((tokens, twice), 1) % (2 * block)
    late = slots_of_late(ids, n_micro, tok_dev, n_expert, block)
    sel_saved = jnp.where(wide & (lane < block), 1.0, 0.0)
    sel_top = jnp.where(late, 1.0, 0.0)
    chosen = jnp.concatenate([sel_saved, sel_top], axis=0).astype(BF16)
    rows = jnp.concatenate(
        [x_ref[0, m] for m in range(n_micro)] + [top_ref[m] for m in range(n_micro)], axis=0
    )
    send_ref[:, 0:feat] = contract(chosen, rows, 0, 0).astype(BF16)
    examples = []
    for m in range(n_micro):
        diagonal = iota((tok_dev, tok_dev), 0) == iota((tok_dev, tok_dev), 1)
        own = jnp.where(diagonal, jnp.broadcast_to(ex_ref[m : m + 1, :], (tok_dev, tok_dev)), 0)
        examples.append(jnp.sum(own, axis=1, keepdims=True) + m * EXM)
    example = jnp.concatenate(examples, axis=0)
    onehot = (example == iota((tokens, META), 1)).astype(BF16)
    group_wide = iota((tokens, twice), 1) // (2 * block * (n_expert // EXPERTS))
    weight_wide = jnp.where(ids[:, 0:1] == group_wide, weights[:, 0:1], 0.0)
    for k in range(1, ids.shape[1]):
        weight_wide = weight_wide + jnp.where(
            ids[:, k : k + 1] == group_wide, weights[:, k : k + 1], 0.0
        )
    comb_wide = (sel_saved * weight_wide).astype(BF16)
    send_ref[:, feat:] = contract(comb_wide, onehot, 0, 0).astype(BF16)


def slots_of_late(ids, n_micro, tok_dev, n_expert, block):
    tokens = n_micro * tok_dev
    lanes = n_expert * 2 * block
    hsplit = n_expert // EXPERTS
    group = iota((tokens, lanes), 1) // (2 * block * hsplit)
    hit = ids[:, 0:1] == group
    for k in range(1, ids.shape[1]):
        hit = hit | (ids[:, k : k + 1] == group)
    row, col = iota((tokens, tokens), 0), iota((tokens, tokens), 1)
    earlier = ((row // tok_dev == col // tok_dev) & (col < row)).astype(F32)
    position = contract(earlier, hit.astype(F32), 1, 0)
    slot = iota((tokens, lanes), 1) % (2 * block) - block
    slot = slot - (iota((tokens, lanes), 0) // tok_dev) * CAP
    return hit & (slot >= 0) & (slot < CAP) & (position.astype(jnp.int32) == slot)


def on_device(
    saved_inputs,
    top_grad,
    expert_ids,
    route_weights,
    example_ids,
    gate_weight,
    up_weight,
    down_weight,
    left_proj,
    right_proj,
):
    n_section = lax.axis_size("section")
    n_expert = lax.axis_size("expert")
    section_id = lax.axis_index("section")
    expert_id = lax.axis_index("expert")
    hsplit = n_expert // EXPERTS
    n_micro, tok_dev, feat = saved_inputs.shape[1:]
    tokens = n_micro * tok_dev
    sketch_dim = left_proj.shape[2]
    flat = sketch_dim * sketch_dim
    used = n_micro * CAP
    extra = -(-flat // feat)
    block = -(-(used + extra) // 8) * 8
    n_rows = n_expert * block
    q_dev = n_micro * EXM * EXPERTS // n_expert

    vmem = pl.BlockSpec(memory_space=pltpu.VMEM)
    send, sel, comb = pl.pallas_call(
        functools.partial(prepare, n_expert, block),
        out_shape=(
            jax.ShapeDtypeStruct((2 * n_rows, feat + META), BF16),
            jax.ShapeDtypeStruct((tokens, n_rows), BF16),
            jax.ShapeDtypeStruct((tokens, n_rows), BF16),
        ),
        in_specs=[vmem] * 5,
        out_specs=(vmem, vmem, vmem),
    )(expert_ids, route_weights, example_ids, saved_inputs, top_grad)
    first = lax.all_to_all(
        send.reshape(n_expert, 2 * block, feat + META),
        "expert",
        split_axis=0,
        concat_axis=0,
        tiled=True,
    )
    x_rows = first[:, :block, :feat].reshape(n_rows, feat)
    meta = first[:, :block, feat:].reshape(n_rows, META)
    rows = first[:, block:, :feat].reshape(n_rows, feat)
    w_gate, w_up, w_down = gate_weight[0], up_weight[0], down_weight[0]
    pre_gate = contract(x_rows, w_gate, 1, 1)
    pre_up = contract(x_rows, w_up, 1, 1)
    sigmoid = jax.nn.sigmoid(pre_gate)
    to_up = pre_gate * sigmoid
    to_gate = pre_up * sigmoid * (1.0 + pre_gate * (1.0 - sigmoid))
    hidden = (to_up * pre_up).astype(BF16)
    left = contract(hidden, left_proj[0], 1, 0).astype(BF16)

    out_grad = top_grad.reshape(tokens, feat)
    right = jnp.zeros((n_rows, sketch_dim), F32)
    own_grad = jnp.zeros((tokens, feat), BF16)
    sketch_rows = None
    for stage in range(n_section):
        mine = section_id == n_section - 1 - stage
        if stage > 0:
            out_grad = lax.ppermute(
                new_grad, "section", [(n_section - stage, n_section - 1 - stage)]
            )
            spread = contract(sel, out_grad, 0, 0).astype(BF16)
            rows = lax.all_to_all(
                spread.reshape(n_expert, block, feat),
                "expert",
                split_axis=0,
                concat_axis=0,
                tiled=True,
            ).reshape(n_rows, feat)
        grad_hidden = contract(rows, w_down, 1, 1)
        grad_gate = (grad_hidden * to_gate).astype(BF16)
        grad_up = (grad_hidden * to_up).astype(BF16)
        part = contract(grad_gate, w_gate, 1, 0) + contract(grad_up, w_up, 1, 0)
        right = jnp.where(mine, contract(rows, right_proj[0], 1, 0), right)
        if stage == n_section - 1:
            lane = jnp.arange(flat, dtype=jnp.int32)
            axis = jnp.arange(sketch_dim, dtype=jnp.int32)
            spread_left = (axis[:, None] == lane[None, :] // sketch_dim).astype(BF16)
            spread_right = (axis[:, None] == lane[None, :] % sketch_dim).astype(BF16)
            right_high = right.astype(BF16)
            right_low = (right - right_high.astype(F32)).astype(BF16)
            outer = contract(left, spread_left, 1, 0) * (
                contract(right_high, spread_right, 1, 0) + contract(right_low, spread_right, 1, 0)
            )
            place = jnp.arange(n_rows, dtype=jnp.int32)
            target = (place // block) * q_dev
            here = (expert_id // hsplit >= target % EXPERTS) & (
                expert_id // hsplit < target % EXPERTS + q_dev
            )
            wanted = jnp.where(here, target // EXPERTS, -1)
            picks = (wanted[:, None] == jnp.arange(META, dtype=jnp.int32)[None, :]).astype(BF16)
            terms = contract(picks, meta, 1, 1)
            for part_no in range(extra):
                at_row = (place % block == used + part_no)[:, None]
                chosen = jnp.where(at_row, terms, 0.0).astype(BF16)
                part = part + contract(
                    chosen, outer[:, part_no * feat : (part_no + 1) * feat].astype(BF16), 1, 0
                )
        back = lax.all_to_all(
            part.astype(BF16).reshape(n_expert, block, feat),
            "expert",
            split_axis=0,
            concat_axis=0,
            tiled=True,
        )
        summed = contract(comb, back.reshape(n_rows, feat), 1, 0)
        new_grad = (out_grad.astype(F32) + summed).astype(BF16)
        own_grad = jnp.where(mine, new_grad, own_grad)
        sketch_rows = back[:, used : used + extra]
    sketch = sketch_rows.reshape(EXPERTS, hsplit, extra * feat).astype(F32).sum(axis=1)[:, :flat]
    start = (expert_id * q_dev) % EXPERTS
    sketch = lax.dynamic_slice_in_dim(sketch, start, q_dev, 0)
    return own_grad.reshape(1, n_micro, tok_dev, feat), sketch[None]


def solution(mesh):
    placed = (
        P("section", None, "expert", None),
        P(None, "expert", None),
        P("section", None, "expert", None),
        P("section", None, "expert", None),
        P(None, "expert"),
        P("section", "expert", None),
        P("section", "expert", None),
        P("section", "expert", None),
        P("section", "expert", None),
        P("section", None, None),
    )
    return jax.shard_map(
        on_device,
        mesh=mesh,
        in_specs=placed,
        out_specs=(P("section", None, "expert", None), P("section", "expert", None)),
        check_vma=False,
    )
```

```python
import functools
import math

import jax
import jax.numpy as jnp
from jax import lax
from jax.experimental import pallas as pl
from jax.experimental.pallas import tpu as pltpu
from jax.sharding import PartitionSpec as P

EXPERTS = 8
EXM = 4
CAP = 3
LANES = 128
TILE = 256
MOST_PERMUTES = 8

F32 = jnp.float32
BF16 = jnp.bfloat16
VMEM = pl.BlockSpec(memory_space=pltpu.VMEM)
HBM = pl.BlockSpec(memory_space=pltpu.HBM)


def contract(a, b, dim_a, dim_b):
    return lax.dot_general(a, b, (((dim_a,), (dim_b,)), ((), ())), preferred_element_type=F32)


def iota(shape, dim):
    return lax.broadcasted_iota(jnp.int32, shape, dim)


def ones_where(mask):
    return jnp.where(mask, 1.0, 0.0).astype(F32)


def partner(device, turn, amount):
    if amount & (amount - 1) == 0:
        return device ^ turn
    return (turn + 2 * amount - device) % amount


def size_of(arrays):
    return sum(a.dtype.itemsize * a.size for a in arrays)


def call(kernel, out_shape, inputs, spec=VMEM, scratch=(), limit=12 << 20):
    return pl.pallas_call(
        kernel,
        out_shape=out_shape,
        in_specs=[spec] * len(inputs),
        out_specs=tuple(VMEM for _ in out_shape),
        scratch_shapes=list(scratch),
        compiler_params=pltpu.CompilerParams(vmem_limit_bytes=limit),
    )(*inputs)


def copy_all(pairs, sems):
    copies = []
    for number, (source, target) in enumerate(pairs):
        copies.append(pltpu.make_async_copy(source, target, sems.at[number]))
        copies[-1].start()
    for copy in copies:
        copy.wait()


def names(fields, top_k, group):
    hit = fields[0:1, :] == group
    for k in range(1, top_k):
        hit = hit | (fields[k : k + 1, :] == group)
    return ones_where(hit)


def prepare(n_section, n_expert, block, ids_hbm, w_hbm, ex_hbm, x_hbm, top_hbm, *refs):
    saved_ref, top_send_ref, slots_ref = refs[:3]
    ids_ref, w_ref, ex_ref, x_ref, top_ref, sems = refs[3:]
    from_hbm = (ids_hbm, w_hbm, ex_hbm, x_hbm, top_hbm)
    copy_all(list(zip(from_hbm, (ids_ref, w_ref, ex_ref, x_ref, top_ref))), sems)
    n_micro, top_k, tok_dev = ids_ref.shape[1:]
    tokens = n_micro * tok_dev
    n_all = n_expert * tokens
    n_fields = 2 * top_k + 1
    feat = x_ref.shape[3]
    section, me = lax.axis_index("section"), lax.axis_index("expert")
    padded = -(-n_fields // 8) * 8
    local = jnp.zeros((padded, tokens), F32)
    packed = jnp.zeros((padded, n_all), F32)
    for m in range(n_micro):
        row = iota((padded, tok_dev), 0)
        example = ex_ref[m : m + 1, :] + m * EXM
        fields = jnp.where(row == 2 * top_k, example.astype(F32), 0.0)
        for k in range(top_k):
            fields = jnp.where(row == k, ids_ref[0, m, k : k + 1, :].astype(F32), fields)
            fields = jnp.where(row == top_k + k, w_ref[0, m, k : k + 1, :].astype(F32), fields)
        here = iota((tok_dev, tokens), 1) == m * tok_dev + iota((tok_dev, tokens), 0)
        local = local + contract(fields, ones_where(here), 1, 0)
        there = me * tokens + m * tok_dev + iota((tok_dev, n_all), 0)
        packed = packed + contract(fields, ones_where(iota((tok_dev, n_all), 1) == there), 1, 0)
    rows = n_expert * block
    group = (iota((rows, tokens), 0) // (block * (n_expert // EXPERTS))).astype(F32)
    hit = names(local, top_k, group)
    early, late = iota((tokens, tokens), 0), iota((tokens, tokens), 1)
    before = ones_where((early // tok_dev == late // tok_dev) & (early < late))
    position = contract(hit, before, 1, 0)
    slot = iota((rows, tokens), 0) % block - CAP * (iota((rows, tokens), 1) // tok_dev)
    fits = (hit > 0.5) & (slot >= 0) & (slot < CAP) & (position == slot.astype(F32))
    slots = ones_where(fits).astype(BF16)
    slots_ref[...] = slots
    saved = jnp.concatenate([x_ref[0, m] for m in range(n_micro)], axis=0)
    saved_ref[...] = contract(slots, saved, 1, 0).astype(BF16)
    for number, (at_row, lanes) in enumerate(field_places(n_fields, n_all, feat, n_micro * CAP)):
        spare = iota((rows, n_all), 0) % block == at_row
        field = jnp.broadcast_to(packed[number : number + 1, :], (rows, n_all))
        kept = saved_ref[:, lanes].astype(F32)
        saved_ref[:, lanes] = jnp.where(spare, field, kept).astype(BF16)
    top = jnp.concatenate([top_ref[m] for m in range(n_micro)], axis=0)
    used = jnp.where(section == n_section - 1, slots, jnp.zeros_like(slots))
    top_send_ref[...] = contract(used, top, 1, 0).astype(BF16)


def field_places(n_fields, n_all, feat, first_row):
    per_row = feat // n_all
    for number in range(n_fields):
        at = number % per_row * n_all
        yield first_row + number // per_row, slice(at, at + n_all)


def collect(block, used, n_fields, x_ref, fields_ref):
    n_all = fields_ref.shape[1]
    rows, feat = x_ref.shape
    total = jnp.zeros(fields_ref.shape, F32)
    for number, (at_row, lanes) in enumerate(field_places(n_fields, n_all, feat, used)):
        spare = iota((rows, n_all), 0) % block == at_row
        kept = jnp.where(spare, x_ref[:, lanes].astype(F32), 0.0)
        field = jnp.sum(kept, axis=0, keepdims=True)
        total = jnp.where(iota(fields_ref.shape, 0) == number, field, total)
    fields_ref[...] = total


def plan(
    n_section, n_expert, n_micro, tok_dev, top_k, block, share, q_dev, *refs
):
    around, refs = refs[:n_section], refs[n_section:]
    comp_ref, place_ref, cols_ref, sketch_ref, over_ref = refs
    n_all = around[0].shape[1]
    tokens = n_micro * tok_dev
    hsplit = n_expert // EXPERTS
    rows = n_expert * block
    section, me = lax.axis_index("section"), lax.axis_index("expert")
    mine, below, above = around[0][...], around[-1][...], around[1 % n_section][...]
    group = (me // hsplit).astype(F32)
    hit = names(mine, top_k, group)
    early, late = iota((n_all, n_all), 0), iota((n_all, n_all), 1)
    before = ones_where(early < late)
    near = ones_where((early // tok_dev == late // tok_dev) & (early < late))
    lane = iota((8, n_all), 1)
    count = contract(jnp.broadcast_to(hit, (8, n_all)), near, 1, 0)
    slot = (lane // tokens) * block + (lane // tok_dev) % n_micro * CAP
    slot = (slot.astype(F32) + count)[0:1, :]
    held = ones_where((iota((rows, n_all), 0).astype(F32) == slot) & (hit > 0.5))
    weight = jnp.zeros((1, n_all), F32)
    for k in range(top_k):
        weight = weight + jnp.where(
            mine[k : k + 1, :] == group, mine[top_k + k : top_k + k + 1, :], 0.0
        )
    first = ones_where((mine[0:1, :] == group) & (me % hsplit == 0))
    column = iota((rows, LANES), 1)
    weight_col = jnp.sum(held * weight, axis=1, keepdims=True)
    first_col = jnp.sum(held * first, axis=1, keepdims=True)
    cols_ref[...] = jnp.where(column == 0, weight_col, jnp.where(column == 1, first_col, 0.0))

    held_b = held.astype(BF16)
    peers = (partner(me, iota((n_expert, n_all), 0), n_expert) // hsplit).astype(F32)
    for other, to_row in ((below, True), (above, False)):
        both = names(other, top_k, peers) * hit
        position = contract(both, before, 1, 0)
        picks = []
        for turn in range(n_expert):
            chosen = position[turn : turn + 1, :] == iota((share, n_all), 0).astype(F32)
            picks.append(ones_where(chosen) * both[turn : turn + 1, :])
        picks = jnp.concatenate(picks, axis=0).astype(BF16)
        if to_row:
            comp_ref[...] = contract(picks, held_b, 1, 1).astype(BF16)
        else:
            place_ref[...] = contract(held_b, picks, 1, 1).astype(BF16)

    place = iota((rows, n_all), 0)
    target = (place // block) * q_dev
    local = me // hsplit
    inside = (local >= target % EXPERTS) & (local < target % EXPERTS + q_dev)
    example = mine[2 * top_k : 2 * top_k + 1, :]
    fits = inside & (example == (target // EXPERTS).astype(F32))
    for part_no in range(sketch_ref.shape[0]):
        at_row = place % block == n_micro * CAP + part_no
        terms = jnp.where(fits & at_row, weight, 0.0).astype(BF16)
        sketch_ref[part_no] = contract(terms, held_b, 1, 1).astype(BF16)

    expert = iota((EXPERTS, n_all), 0).astype(F32)
    most = jnp.zeros((1, 1), F32)
    upper = names(mine, top_k, expert)
    for turn in range(1, n_section + 1):
        lower, upper = upper, names(around[turn % n_section][...], top_k, expert)
        shared = jnp.max(contract(upper, lower, 1, 1), axis=(0, 1), keepdims=True)
        wraps = (section + turn) % n_section == 0
        most = jnp.maximum(most, jnp.where(wraps, 0.0, shared))
    over_ref[...] = jnp.broadcast_to(most, over_ref.shape)


def forward(
    x_ref, gate_hbm, up_hbm, down_hbm, left_hbm, right_hbm,
    to_gate_ref, to_up_ref, left_ref, gate_ref, up_ref, down_ref, left_map, right_map, sems,
):
    hidden = gate_ref.shape[1]
    tile = math.gcd(hidden, TILE)
    pairs = [(left_hbm, left_map)]
    for at in range(0, hidden, tile):
        part = pl.ds(at, tile)
        pairs.append((gate_hbm.at[:, part, :], gate_ref.at[:, part, :]))
        pairs.append((up_hbm.at[:, part, :], up_ref.at[:, part, :]))
    for at in range(0, hidden, tile):
        part = pl.ds(at, tile)
        pairs.append((down_hbm.at[:, part, :], down_ref.at[:, part, :]))
    pairs.append((right_hbm, right_map))
    copies = [pltpu.make_async_copy(a, b, sems.at[i]) for i, (a, b) in enumerate(pairs)]
    for copy in copies:
        copy.start()
    copies.pop(0).wait()
    left = jnp.zeros(left_ref.shape, F32)
    for at in range(0, hidden, tile):
        part = slice(at, at + tile)
        copies.pop(0).wait()
        gate = contract(x_ref[...], gate_ref[0, part, :], 1, 1)
        copies.pop(0).wait()
        up = contract(x_ref[...], up_ref[0, part, :], 1, 1)
        sigmoid = jax.nn.sigmoid(gate)
        silu = gate * sigmoid
        to_up_ref[:, part] = silu
        to_gate_ref[:, part] = up * sigmoid * (1.0 + gate * (1.0 - sigmoid))
        left = left + contract((silu * up).astype(BF16), left_map[0, :, part], 1, 1)
    left_ref[...] = left.astype(BF16)
    for copy in copies:
        copy.wait()


def layer(n_arrived, n_sent, n_before, stage, n_section, n_extra, *refs):
    refs = list(refs)
    take = lambda amount: [refs.pop(0) for _ in range(amount)]
    arrived = take(n_arrived)
    place = take(1)[0] if n_arrived > 1 else None
    to_gate, to_up, down, gate, up, cols = take(6)
    comp = take(1)[0] if n_sent else None
    rows_before, part_before = take(2) if n_before else (None, None)
    if not n_sent:
        left_ref, right_proj, sketch = take(3)
    sent = take(n_sent)
    part_ref, rows_ref = take(2) if n_sent else take(1) + [None]
    grad_gate, grad_up, rows_now = take(3)
    feat = rows_now.shape[1]
    live = lax.axis_index("section") == n_section - 1 - stage

    @pl.when(live)
    def _():
        if n_arrived > 1:
            pieces = jnp.concatenate([ref[...].astype(F32) for ref in arrived], axis=0)
            rows = contract(place[...], pieces.astype(BF16), 1, 0).astype(BF16)
        else:
            rows = arrived[0][...]
        rows_now[...] = rows
        tile = math.gcd(grad_gate.shape[1], TILE)
        for at in range(0, grad_gate.shape[1], tile):
            part = slice(at, at + tile)
            grad_hidden = contract(rows, down[0, part, :], 1, 1)
            grad_gate[:, part] = (grad_hidden * to_gate[:, part]).astype(BF16)
            grad_up[:, part] = (grad_hidden * to_up[:, part]).astype(BF16)
        weight, first = cols[:, 0:1], cols[:, 1:2]
        for at in range(0, feat, TILE):
            part = slice(at, at + TILE)
            total = contract(grad_gate[...], gate[0, :, part], 1, 0)
            total = total + contract(grad_up[...], up[0, :, part], 1, 0)
            total = total * weight + rows[:, part].astype(F32) * first
            total = total.astype(BF16)
            part_ref[:, part] = total
            if n_sent:
                chosen = contract(comp[...], total, 1, 0)
                share = chosen.shape[0] // n_sent
                for turn in range(n_sent):
                    sent[turn][:, part] = chosen[turn * share : (turn + 1) * share].astype(BF16)

    @pl.when(jnp.logical_not(live))
    def _():
        if n_before:
            rows_now[...] = rows_before[...]
            part_ref[...] = part_before[...]
        else:
            rows_now[...] = jnp.zeros(rows_now.shape, BF16)
            part_ref[...] = jnp.zeros(part_ref.shape, BF16)

    if n_sent:
        rows_ref[...] = rows_now[...]
        return
    right = contract(rows_now[...], right_proj[0], 1, 1)
    high = right.astype(BF16)
    low = (right - high.astype(F32)).astype(BF16)
    left = left_ref[...]
    size = left.shape[1]
    lane, axis = iota((size, TILE), 1), iota((size, TILE), 0)
    over_right = ones_where(axis == lane % size).astype(BF16)
    right = contract(high, over_right, 1, 0) + contract(low, over_right, 1, 0)
    for number in range(n_extra):
        for at in range(0, feat, TILE):
            part = slice(at, at + TILE)
            over_left = ones_where(axis == (number * feat + at + lane) // size).astype(BF16)
            outer = contract(left, over_left, 1, 0) * right
            terms = contract(sketch[number], outer.astype(BF16), 1, 0)
            part_ref[:, part] = (part_ref[:, part].astype(F32) + terms).astype(BF16)


def finish(n_expert, block, used, n_extra, q_dev, back_ref, slots_ref, grad_ref, sketch_ref):
    me = lax.axis_index("expert")
    hsplit = n_expert // EXPERTS
    n_micro, tok_dev, feat = grad_ref.shape[1:]
    rows = n_expert * block
    start = (me * q_dev) % EXPERTS
    group = iota((q_dev, rows), 1) // (block * hsplit)
    owner = group == start + iota((q_dev, rows), 0)
    back = back_ref[...]
    total = contract(slots_ref[...], back, 0, 0)
    for m in range(n_micro):
        grad_ref[0, m] = total[m * tok_dev : (m + 1) * tok_dev].astype(BF16)
    for number in range(n_extra):
        at_row = iota((q_dev, rows), 1) % block == used + number
        picks = ones_where(owner & at_row).astype(BF16)
        sketch_ref[0, :, number * feat : (number + 1) * feat] = contract(picks, back, 1, 0)


def send_down(blocks, section, n_expert):
    window = 5
    far, near = list(range(n_expert - 1, n_expert // 2 - 1, -1)), list(range(n_expert // 2))
    near[0:2] = near[1::-1]
    order = []
    while far or near:
        for some, amount in ((far, 1), (near, 1), (far, 1), (near, 1), (far, 2), (near, 2)):
            order += some[:amount]
            del some[:amount]
    freed = [3, 1, 0, 2, 4] + list(range(5, n_expert))
    arrived = [None] * n_expert
    for place, turn in enumerate(order):
        pairs = [
            (section * n_expert + e, (section - 1) * n_expert + partner(e, turn, n_expert))
            for e in range(n_expert)
        ]
        block = blocks[turn]
        if place >= window:
            earlier = order[freed[place - window]]
            block, arrived[earlier] = lax.optimization_barrier((block, arrived[earlier]))
        arrived[turn] = lax.ppermute(block, ("section", "expert"), pairs)
    return arrived


def by_owners(block, used, n_extra, q_dev, arrays, slots, x_rows, top_rows, cols, sketch):
    top_grad, gate_weight, up_weight, down_weight, left_proj, right_proj = arrays
    n_section, n_expert = lax.axis_size("section"), lax.axis_size("expert")
    section = lax.axis_index("section")
    n_micro, tok_dev, feat = top_grad.shape
    tokens = n_micro * tok_dev
    n_rows = n_expert * block

    def exchange(rows):
        blocks = rows.reshape(n_expert, block, feat)
        blocks = lax.all_to_all(blocks, "expert", split_axis=0, concat_axis=0, tiled=True)
        return blocks.reshape(n_rows, feat)

    gate, up, down = gate_weight[0], up_weight[0], down_weight[0]
    pre_gate = contract(x_rows, gate, 1, 1)
    pre_up = contract(x_rows, up, 1, 1)
    sigmoid = jax.nn.sigmoid(pre_gate)
    to_up = pre_gate * sigmoid
    to_gate = pre_up * sigmoid * (1.0 + pre_gate * (1.0 - sigmoid))
    left = contract((to_up * pre_up).astype(BF16), left_proj[0], 1, 0).astype(BF16)
    size = left.shape[1]
    rows = top_rows
    right = jnp.zeros((n_rows, size), F32)
    own = jnp.zeros((tokens, feat), BF16)
    for stage in range(n_section):
        live = section == n_section - 1 - stage
        if stage > 0:
            hop = [(n_section - stage, n_section - 1 - stage)]
            out_grad = lax.ppermute(new_grad, "section", hop)
            rows = exchange(contract(slots, out_grad, 1, 0).astype(BF16))
        grad_hidden = contract(rows, down, 1, 1)
        part = contract((grad_hidden * to_gate).astype(BF16), gate, 1, 0)
        part = part + contract((grad_hidden * to_up).astype(BF16), up, 1, 0)
        part = part * cols[:, 0:1] + rows.astype(F32) * cols[:, 1:2]
        right = right + jnp.where(live, contract(rows, right_proj[0], 1, 0), 0.0)
        back = exchange(part.astype(BF16))
        new_grad = contract(slots, back, 0, 0).astype(BF16)
        own = jnp.where(live, new_grad, own)
    outer = (left.astype(F32)[:, :, None] * right[:, None, :]).astype(BF16)
    outer = outer.reshape(n_rows, n_extra * feat)
    terms = jnp.zeros((n_rows, feat), F32)
    for number in range(n_extra):
        here = outer[:, number * feat : (number + 1) * feat]
        terms = terms + contract(sketch[number], here, 1, 0)
    back = exchange(terms.astype(BF16)).reshape(EXPERTS, n_expert // EXPERTS, block, feat)
    back = back[:, :, used : used + n_extra].astype(F32).sum(axis=1)
    back = back.reshape(EXPERTS, n_extra * feat)
    start = (lax.axis_index("expert") * q_dev) % EXPERTS
    found = lax.dynamic_slice_in_dim(back, start, q_dev, 0)
    return own.reshape(1, n_micro, tok_dev, feat), found[None]


def on_device(
    saved_inputs,
    top_grad,
    expert_ids,
    route_weights,
    example_ids,
    gate_weight,
    up_weight,
    down_weight,
    left_proj,
    right_proj,
):
    n_section = lax.axis_size("section")
    n_expert = lax.axis_size("expert")
    n_micro, tok_dev, feat = saved_inputs.shape[1:]
    top_k = expert_ids.shape[3]
    hidden = gate_weight.shape[1]
    tokens = n_micro * tok_dev
    sketch_dim = left_proj.shape[2]
    used = n_micro * CAP
    n_extra = sketch_dim * sketch_dim // feat
    block = -(-(used + n_extra) // 8) * 8
    n_rows = n_expert * block
    q_dev = n_micro * EXM * EXPERTS // n_expert
    share = -(-(n_expert * used // 2) // 8) * 8
    n_picks = n_expert * share

    def shape(*dims, dtype=BF16):
        return jax.ShapeDtypeStruct(dims, dtype)

    arrays = (
        expert_ids.transpose(0, 1, 3, 2),
        route_weights.transpose(0, 1, 3, 2),
        example_ids,
        saved_inputs,
        top_grad,
    )
    saved_send, top_send, slots = call(
        functools.partial(prepare, n_section, n_expert, block),
        (shape(n_rows, feat), shape(n_rows, feat), shape(n_rows, tokens)),
        arrays,
        HBM,
        [pltpu.VMEM(a.shape, a.dtype) for a in arrays] + [pltpu.SemaphoreType.DMA((5,))],
    )

    def exchange(rows):
        blocks = rows.reshape(n_expert, block, feat)
        blocks = lax.all_to_all(blocks, "expert", split_axis=0, concat_axis=0, tiled=True)
        return blocks.reshape(n_rows, feat)

    x_rows = exchange(saved_send)
    (fields,) = call(
        functools.partial(collect, block, used, 2 * top_k + 1),
        (shape(-(-(2 * top_k + 1) // 8) * 8, n_expert * tokens, dtype=F32),),
        (x_rows,),
    )
    around = [fields]
    for turn in range(1, n_section):
        pairs = [(i, (i - turn) % n_section) for i in range(n_section)]
        around.append(lax.ppermute(fields, "section", pairs))
    top_rows = exchange(top_send)
    kept = (
        gate_weight,
        up_weight,
        down_weight,
        left_proj.transpose(0, 2, 1),
        right_proj.transpose(0, 2, 1),
    )
    kept, top_rows = lax.optimization_barrier((kept, top_rows))
    to_gate, to_up, left, gate, up, down, left_map, right_map = pl.pallas_call(
        forward,
        out_shape=(
            shape(n_rows, hidden, dtype=F32),
            shape(n_rows, hidden, dtype=F32),
            shape(n_rows, sketch_dim),
        )
        + tuple(pltpu.VMEM(a.shape, a.dtype) for a in kept),
        in_specs=[VMEM] + [HBM] * len(kept),
        out_specs=(VMEM,) * (3 + len(kept)),
        scratch_shapes=[pltpu.SemaphoreType.DMA((2 + 3 * (hidden // math.gcd(hidden, TILE)),))],
        compiler_params=pltpu.CompilerParams(vmem_limit_bytes=40 << 20),
    )(x_rows, *kept)
    comp, place, cols, sketch, over = call(
        functools.partial(
            plan, n_section, n_expert, n_micro, tok_dev, top_k, block, share, q_dev
        ),
        (
            shape(n_picks, n_rows),
            shape(n_rows, n_picks),
            shape(n_rows, LANES, dtype=F32),
            shape(n_extra, n_rows, n_rows),
            shape(8, LANES, dtype=F32),
        ),
        around,
        limit=(12 << 20) + 16 * n_rows * n_picks,
    )

    raw = (top_grad, gate_weight, up_weight, down_weight, left_proj, right_proj)

    def crowded(*_):
        return by_owners(
            block, used, n_extra, q_dev, raw, slots, x_rows, top_rows, cols, sketch
        )

    if n_expert > MOST_PERMUTES:
        return crowded()

    rows, part = None, None
    arrived = [top_rows]
    for stage in range(n_section):
        last = stage == n_section - 1
        inputs = list(arrived)
        if stage > 0:
            inputs += [place]
        inputs += [to_gate, to_up, down, gate, up, cols]
        if last:
            inputs += [rows, part, left, right_map, sketch]
            out = (shape(n_rows, feat),)
        else:
            inputs += [comp] + ([rows, part] if stage > 0 else [])
            out = tuple(shape(share, feat) for _ in range(n_expert))
            out += (shape(n_rows, feat), shape(n_rows, feat))
        kernel = functools.partial(
            layer,
            len(arrived),
            0 if last else n_expert,
            stage > 0,
            stage,
            n_section,
            n_extra,
        )
        results = pl.pallas_call(
            kernel,
            out_shape=out,
            in_specs=[VMEM] * len(inputs),
            out_specs=tuple(VMEM for _ in out),
            scratch_shapes=[
                pltpu.VMEM((n_rows, hidden), BF16),
                pltpu.VMEM((n_rows, hidden), BF16),
                pltpu.VMEM((n_rows, feat), BF16),
            ],
            compiler_params=pltpu.CompilerParams(
                vmem_limit_bytes=(12 << 20) + 2 * size_of(out) + 2 * size_of(arrived)
            ),
        )(*inputs)
        if last:
            back = exchange(results[0])
            break
        part, rows = results[-2:]
        arrived = send_down(results[:n_expert], n_section - 1 - stage, n_expert)

    def direct(*_):
        return call(
            functools.partial(finish, n_expert, block, used, n_extra, q_dev),
            (
                shape(1, n_micro, tok_dev, feat),
                shape(1, q_dev, sketch_dim * sketch_dim, dtype=F32),
            ),
            (back, slots),
        )

    return lax.cond(over[0, 0] > share, crowded, direct)


def solution(mesh):
    placed = (
        P("section", None, "expert", None),
        P(None, "expert", None),
        P("section", None, "expert", None),
        P("section", None, "expert", None),
        P(None, "expert"),
        P("section", "expert", None),
        P("section", "expert", None),
        P("section", "expert", None),
        P("section", "expert", None),
        P("section", None, None),
    )
    return jax.shard_map(
        on_device,
        mesh=mesh,
        in_specs=placed,
        out_specs=(P("section", None, "expert", None), P("section", "expert", None)),
        check_vma=False,
    )
```

```python
import functools
import math

import jax
import jax.numpy as jnp
from jax import lax
from jax.experimental import pallas as pl
from jax.experimental.pallas import tpu as pltpu
from jax.sharding import PartitionSpec as P

EXPERTS = 8
EXM = 4
CAP = 3
LANES = 128
TILE = 256
MOST_PERMUTES = 8
NARROW = (1536, 1)
WIDEN = (2048, 1)
FORWARD = 512
HALVES = 2

F32 = jnp.float32
BF16 = jnp.bfloat16
VMEM = pl.BlockSpec(memory_space=pltpu.VMEM)
HBM = pl.BlockSpec(memory_space=pltpu.HBM)


def contract(a, b, dim_a, dim_b):
    return lax.dot_general(a, b, (((dim_a,), (dim_b,)), ((), ())), preferred_element_type=F32)


def iota(shape, dim):
    return lax.broadcasted_iota(jnp.int32, shape, dim)


def ones_where(mask):
    return jnp.where(mask, 1.0, 0.0).astype(F32)


def partner(device, turn, amount):
    if amount & (amount - 1) == 0:
        return device ^ turn
    return (turn + 2 * amount - device) % amount


def size_of(arrays):
    return sum(a.dtype.itemsize * a.size for a in arrays)


def over_tiles(size, shape, body, start=0):
    tile, together = math.gcd(size, shape[0]), shape[1]

    def step(number, carry):
        body(pl.ds(pl.multiple_of(start + number * tile, tile), tile))
        return carry

    if size == tile:
        body(pl.ds(start, tile))
        return
    lax.fori_loop(0, size // tile, step, 0, unroll=math.gcd(size // tile, together))


def call(kernel, out_shape, inputs, spec=VMEM, scratch=(), limit=12 << 20):
    return pl.pallas_call(
        kernel,
        out_shape=out_shape,
        in_specs=[spec] * len(inputs),
        out_specs=tuple(VMEM for _ in out_shape),
        scratch_shapes=list(scratch),
        compiler_params=pltpu.CompilerParams(vmem_limit_bytes=limit),
    )(*inputs)


def copy_all(pairs, sems):
    copies = []
    for number, (source, target) in enumerate(pairs):
        copies.append(pltpu.make_async_copy(source, target, sems.at[number]))
        copies[-1].start()
    for copy in copies:
        copy.wait()


def names(fields, top_k, group):
    hit = fields[0:1, :] == group
    for k in range(1, top_k):
        hit = hit | (fields[k : k + 1, :] == group)
    return ones_where(hit)


def prepare(n_section, n_expert, block, ids_hbm, w_hbm, ex_hbm, x_hbm, top_hbm, *refs):
    saved_ref, top_send_ref, slots_ref = refs[:3]
    ids_ref, w_ref, ex_ref, x_ref, top_ref, sems = refs[3:]
    from_hbm = (ids_hbm, w_hbm, ex_hbm, x_hbm, top_hbm)
    copy_all(list(zip(from_hbm, (ids_ref, w_ref, ex_ref, x_ref, top_ref))), sems)
    n_micro, top_k, tok_dev = ids_ref.shape[1:]
    tokens = n_micro * tok_dev
    n_all = n_expert * tokens
    n_fields = 2 * top_k + 1
    feat = x_ref.shape[3]
    section, me = lax.axis_index("section"), lax.axis_index("expert")
    padded = -(-n_fields // 8) * 8
    local = jnp.zeros((padded, tokens), F32)
    packed = jnp.zeros((padded, n_all), F32)
    for m in range(n_micro):
        row = iota((padded, tok_dev), 0)
        example = ex_ref[m : m + 1, :] + m * EXM
        fields = jnp.where(row == 2 * top_k, example.astype(F32), 0.0)
        for k in range(top_k):
            fields = jnp.where(row == k, ids_ref[0, m, k : k + 1, :].astype(F32), fields)
            fields = jnp.where(row == top_k + k, w_ref[0, m, k : k + 1, :].astype(F32), fields)
        here = iota((tok_dev, tokens), 1) == m * tok_dev + iota((tok_dev, tokens), 0)
        local = local + contract(fields, ones_where(here), 1, 0)
        there = me * tokens + m * tok_dev + iota((tok_dev, n_all), 0)
        packed = packed + contract(fields, ones_where(iota((tok_dev, n_all), 1) == there), 1, 0)
    rows = n_expert * block
    group = (iota((rows, tokens), 0) // (block * (n_expert // EXPERTS))).astype(F32)
    hit = names(local, top_k, group)
    early, late = iota((tokens, tokens), 0), iota((tokens, tokens), 1)
    before = ones_where((early // tok_dev == late // tok_dev) & (early < late))
    position = contract(hit, before, 1, 0)
    slot = iota((rows, tokens), 0) % block - CAP * (iota((rows, tokens), 1) // tok_dev)
    fits = (hit > 0.5) & (slot >= 0) & (slot < CAP) & (position == slot.astype(F32))
    slots = ones_where(fits).astype(BF16)
    slots_ref[...] = slots
    saved = jnp.concatenate([x_ref[0, m] for m in range(n_micro)], axis=0)
    saved_ref[...] = contract(slots, saved, 1, 0).astype(BF16)
    for number, (at_row, lanes) in enumerate(field_places(n_fields, n_all, feat, n_micro * CAP)):
        spare = iota((rows, n_all), 0) % block == at_row
        field = jnp.broadcast_to(packed[number : number + 1, :], (rows, n_all))
        kept = saved_ref[:, lanes].astype(F32)
        saved_ref[:, lanes] = jnp.where(spare, field, kept).astype(BF16)
    top = jnp.concatenate([top_ref[m] for m in range(n_micro)], axis=0)
    used = jnp.where(section == n_section - 1, slots, jnp.zeros_like(slots))
    top_send_ref[...] = contract(used, top, 1, 0).astype(BF16)


def field_places(n_fields, n_all, feat, first_row):
    per_row = feat // n_all
    for number in range(n_fields):
        at = number % per_row * n_all
        yield first_row + number // per_row, slice(at, at + n_all)


def collect(block, used, n_fields, x_ref, fields_ref):
    n_all = fields_ref.shape[1]
    rows, feat = x_ref.shape
    total = jnp.zeros(fields_ref.shape, F32)
    for number, (at_row, lanes) in enumerate(field_places(n_fields, n_all, feat, used)):
        spare = iota((rows, n_all), 0) % block == at_row
        kept = jnp.where(spare, x_ref[:, lanes].astype(F32), 0.0)
        field = jnp.sum(kept, axis=0, keepdims=True)
        total = jnp.where(iota(fields_ref.shape, 0) == number, field, total)
    fields_ref[...] = total


def plan(
    n_section, n_expert, n_micro, tok_dev, top_k, block, share, q_dev, *refs
):
    around, refs = refs[:n_section], refs[n_section:]
    comp_ref, place_ref, cols_ref, sketch_ref, over_ref = refs
    n_all = around[0].shape[1]
    tokens = n_micro * tok_dev
    hsplit = n_expert // EXPERTS
    rows = n_expert * block
    section, me = lax.axis_index("section"), lax.axis_index("expert")
    mine, below, above = around[0][...], around[-1][...], around[1 % n_section][...]
    group = (me // hsplit).astype(F32)
    hit = names(mine, top_k, group)
    early, late = iota((n_all, n_all), 0), iota((n_all, n_all), 1)
    before = ones_where(early < late)
    near = ones_where((early // tok_dev == late // tok_dev) & (early < late))
    lane = iota((8, n_all), 1)
    count = contract(jnp.broadcast_to(hit, (8, n_all)), near, 1, 0)
    slot = (lane // tokens) * block + (lane // tok_dev) % n_micro * CAP
    slot = (slot.astype(F32) + count)[0:1, :]
    held = ones_where((iota((rows, n_all), 0).astype(F32) == slot) & (hit > 0.5))
    weight = jnp.zeros((1, n_all), F32)
    for k in range(top_k):
        weight = weight + jnp.where(
            mine[k : k + 1, :] == group, mine[top_k + k : top_k + k + 1, :], 0.0
        )
    first = ones_where((mine[0:1, :] == group) & (me % hsplit == 0))
    column = iota((rows, LANES), 1)
    weight_col = jnp.sum(held * weight, axis=1, keepdims=True)
    first_col = jnp.sum(held * first, axis=1, keepdims=True)
    cols_ref[...] = jnp.where(column == 0, weight_col, jnp.where(column == 1, first_col, 0.0))

    held_b = held.astype(BF16)
    peers = (partner(me, iota((n_expert, n_all), 0), n_expert) // hsplit).astype(F32)
    for other, to_row in ((below, True), (above, False)):
        both = names(other, top_k, peers) * hit
        position = contract(both, before, 1, 0)
        picks = []
        for turn in range(n_expert):
            chosen = position[turn : turn + 1, :] == iota((share, n_all), 0).astype(F32)
            picks.append(ones_where(chosen) * both[turn : turn + 1, :])
        picks = jnp.concatenate(picks, axis=0).astype(BF16)
        if to_row:
            comp_ref[...] = contract(picks, held_b, 1, 1).astype(BF16)
        else:
            place_ref[...] = contract(held_b, picks, 1, 1).astype(BF16)

    place = iota((rows, n_all), 0)
    target = (place // block) * q_dev
    local = me // hsplit
    inside = (local >= target % EXPERTS) & (local < target % EXPERTS + q_dev)
    example = mine[2 * top_k : 2 * top_k + 1, :]
    fits = inside & (example == (target // EXPERTS).astype(F32))
    for part_no in range(sketch_ref.shape[0]):
        at_row = place % block == n_micro * CAP + part_no
        terms = jnp.where(fits & at_row, weight, 0.0).astype(BF16)
        sketch_ref[part_no] = contract(terms, held_b, 1, 1).astype(BF16)

    expert = iota((EXPERTS, n_all), 0).astype(F32)
    most = jnp.zeros((1, 1), F32)
    upper = names(mine, top_k, expert)
    for turn in range(1, n_section + 1):
        lower, upper = upper, names(around[turn % n_section][...], top_k, expert)
        shared = jnp.max(contract(upper, lower, 1, 1), axis=(0, 1), keepdims=True)
        wraps = (section + turn) % n_section == 0
        most = jnp.maximum(most, jnp.where(wraps, 0.0, shared))
    over_ref[...] = jnp.broadcast_to(most, over_ref.shape)


def forward(
    x_ref, gate_hbm, up_hbm, left_hbm, to_gate_ref, to_up_ref, left_ref, gate_ref, up_ref, left_map, sems
):
    hidden = to_gate_ref.shape[1]
    tile = math.gcd(hidden, FORWARD)
    first = pltpu.make_async_copy(left_hbm, left_map, sems.at[0])
    first.start()
    copies = []
    for number in range(hidden // tile):
        part = pl.ds(number * tile, tile)
        for source, target in ((gate_hbm, gate_ref), (up_hbm, up_ref)):
            sem = sems.at[len(copies) + 1]
            copies.append(
                pltpu.make_async_copy(source.at[:, part, :], target.at[:, part, :], sem)
            )
            copies[-1].start()
    first.wait()
    left = jnp.zeros(left_ref.shape, F32)
    for number in range(hidden // tile):
        part = slice(number * tile, (number + 1) * tile)
        copies[2 * number].wait()
        gate = contract(x_ref[...], gate_ref[0, part, :], 1, 1)
        copies[2 * number + 1].wait()
        up = contract(x_ref[...], up_ref[0, part, :], 1, 1)
        sigmoid = jax.nn.sigmoid(gate)
        silu = gate * sigmoid
        to_up_ref[:, part] = silu
        to_gate_ref[:, part] = up * sigmoid * (1.0 + gate * (1.0 - sigmoid))
        left = left + contract((silu * up).astype(BF16), left_map[0, :, part], 1, 1)
    left_ref[...] = left.astype(BF16)


def layer(n_arrived, n_sent, n_before, stage, n_section, n_extra, *refs):
    refs = list(refs)
    take = lambda amount: [refs.pop(0) for _ in range(amount)]
    arrived = take(n_arrived)
    place = take(1)[0] if n_arrived > 1 else None
    stored, cols = take(5), take(1)[0]
    comp = take(1)[0] if n_sent else None
    rows_before, part_before = take(2) if n_before else (None, None)
    if not n_sent:
        left_ref, right_proj, sketch = take(3)
    sent = take(n_sent)
    part_ref, rows_ref = take(2) if n_sent else take(1) + [None]
    kept = stored if stage else take(5)
    down, to_gate, to_up, gate, up = kept
    grad_gate, grad_up, rows_now = take(3)
    feat = rows_now.shape[1]
    halves = [slice(0, feat)]
    copies = []
    if not stage:
        halves = [slice(i * feat // HALVES, (i + 1) * feat // HALVES) for i in range(HALVES)]
        pairs = [(stored[i], kept[i]) for i in range(3)]
        for half in halves:
            lanes = pl.ds(half.start, half.stop - half.start)
            pairs += [(stored[i].at[:, :, lanes], kept[i].at[:, :, lanes]) for i in (3, 4)]
        copies = [pltpu.make_async_copy(a, b, refs[0].at[i]) for i, (a, b) in enumerate(pairs)]
        for copy in copies:
            copy.start()
    live = lax.axis_index("section") == n_section - 1 - stage

    @pl.when(live)
    def _():
        if n_arrived > 1:
            pieces = jnp.concatenate([ref[...].astype(F32) for ref in arrived], axis=0)
            rows = contract(place[...], pieces.astype(BF16), 1, 0).astype(BF16)
        else:
            rows = arrived[0][...]
        rows_now[...] = rows
        for copy in copies[:3]:
            copy.wait()

        def narrow(part):
            grad_hidden = contract(rows_now[...], down[0, part, :], 1, 1)
            grad_gate[:, part] = (grad_hidden * to_gate[:, part]).astype(BF16)
            grad_up[:, part] = (grad_hidden * to_up[:, part]).astype(BF16)

        over_tiles(grad_gate.shape[1], NARROW, narrow)

        def widen(part):
            total = contract(grad_gate[...], gate[0, :, part], 1, 0)
            total = total + contract(grad_up[...], up[0, :, part], 1, 0)
            kept = rows_now[:, part].astype(F32) * cols[:, 1:2]
            total = (total * cols[:, 0:1] + kept).astype(BF16)
            part_ref[:, part] = total
            if n_sent:
                chosen = contract(comp[...], total, 1, 0)
                share = chosen.shape[0] // n_sent
                for turn in range(n_sent):
                    sent[turn][:, part] = chosen[turn * share : (turn + 1) * share].astype(BF16)

        for number, half in enumerate(halves):
            for copy in copies[3 + 2 * number : 5 + 2 * number]:
                copy.wait()
            over_tiles(half.stop - half.start, WIDEN, widen, half.start)

    @pl.when(jnp.logical_not(live))
    def _():
        for copy in copies:
            copy.wait()
        if n_before:
            rows_now[...] = rows_before[...]
            part_ref[...] = part_before[...]
        else:
            rows_now[...] = jnp.zeros(rows_now.shape, BF16)
            part_ref[...] = jnp.zeros(part_ref.shape, BF16)

    if n_sent:
        rows_ref[...] = rows_now[...]
        return
    right = contract(rows_now[...], right_proj[0], 1, 1)
    high = right.astype(BF16)
    low = (right - high.astype(F32)).astype(BF16)
    left = left_ref[...]
    size = left.shape[1]
    lane, axis = iota((size, TILE), 1), iota((size, TILE), 0)
    over_right = ones_where(axis == lane % size).astype(BF16)
    right = contract(high, over_right, 1, 0) + contract(low, over_right, 1, 0)
    for number in range(n_extra):

        def add_terms(part, number=number):
            over_left = ones_where(axis == (number * feat + part.start + lane) // size)
            outer = contract(left, over_left.astype(BF16), 1, 0) * right
            terms = contract(sketch[number], outer.astype(BF16), 1, 0)
            part_ref[:, part] = (part_ref[:, part].astype(F32) + terms).astype(BF16)

        over_tiles(feat, (TILE, 2), add_terms)


def finish(n_expert, block, used, n_extra, q_dev, back_ref, slots_ref, grad_ref, sketch_ref):
    me = lax.axis_index("expert")
    hsplit = n_expert // EXPERTS
    n_micro, tok_dev, feat = grad_ref.shape[1:]
    rows = n_expert * block
    start = (me * q_dev) % EXPERTS
    group = iota((q_dev, rows), 1) // (block * hsplit)
    owner = group == start + iota((q_dev, rows), 0)
    back = back_ref[...]
    total = contract(slots_ref[...], back, 0, 0)
    for m in range(n_micro):
        grad_ref[0, m] = total[m * tok_dev : (m + 1) * tok_dev].astype(BF16)
    for number in range(n_extra):
        at_row = iota((q_dev, rows), 1) % block == used + number
        picks = ones_where(owner & at_row).astype(BF16)
        sketch_ref[0, :, number * feat : (number + 1) * feat] = contract(picks, back, 1, 0)


def send_down(blocks, section, n_expert):
    window = 5
    far, near = list(range(n_expert - 1, n_expert // 2 - 1, -1)), list(range(n_expert // 2))
    near[0:2] = near[1::-1]
    order = []
    while far or near:
        for some, amount in ((far, 1), (near, 1), (far, 1), (near, 1), (far, 2), (near, 2)):
            order += some[:amount]
            del some[:amount]
    freed = [3, 1, 0, 2, 4] + list(range(5, n_expert))
    arrived = [None] * n_expert
    for place, turn in enumerate(order):
        pairs = [
            (section * n_expert + e, (section - 1) * n_expert + partner(e, turn, n_expert))
            for e in range(n_expert)
        ]
        block = blocks[turn]
        if place >= window:
            earlier = order[freed[place - window]]
            block, arrived[earlier] = lax.optimization_barrier((block, arrived[earlier]))
        arrived[turn] = lax.ppermute(block, ("section", "expert"), pairs)
    return arrived


def by_owners(block, used, n_extra, q_dev, arrays, slots, x_rows, top_rows, cols, sketch):
    top_grad, gate_weight, up_weight, down_weight, left_proj, right_proj = arrays
    n_section, n_expert = lax.axis_size("section"), lax.axis_size("expert")
    section = lax.axis_index("section")
    n_micro, tok_dev, feat = top_grad.shape
    tokens = n_micro * tok_dev
    n_rows = n_expert * block

    def exchange(rows):
        blocks = rows.reshape(n_expert, block, feat)
        blocks = lax.all_to_all(blocks, "expert", split_axis=0, concat_axis=0, tiled=True)
        return blocks.reshape(n_rows, feat)

    gate, up, down = gate_weight[0], up_weight[0], down_weight[0]
    pre_gate = contract(x_rows, gate, 1, 1)
    pre_up = contract(x_rows, up, 1, 1)
    sigmoid = jax.nn.sigmoid(pre_gate)
    to_up = pre_gate * sigmoid
    to_gate = pre_up * sigmoid * (1.0 + pre_gate * (1.0 - sigmoid))
    left = contract((to_up * pre_up).astype(BF16), left_proj[0], 1, 0).astype(BF16)
    size = left.shape[1]
    rows = top_rows
    right = jnp.zeros((n_rows, size), F32)
    own = jnp.zeros((tokens, feat), BF16)
    for stage in range(n_section):
        live = section == n_section - 1 - stage
        if stage > 0:
            hop = [(n_section - stage, n_section - 1 - stage)]
            out_grad = lax.ppermute(new_grad, "section", hop)
            rows = exchange(contract(slots, out_grad, 1, 0).astype(BF16))
        grad_hidden = contract(rows, down, 1, 1)
        part = contract((grad_hidden * to_gate).astype(BF16), gate, 1, 0)
        part = part + contract((grad_hidden * to_up).astype(BF16), up, 1, 0)
        part = part * cols[:, 0:1] + rows.astype(F32) * cols[:, 1:2]
        right = right + jnp.where(live, contract(rows, right_proj[0], 1, 0), 0.0)
        back = exchange(part.astype(BF16))
        new_grad = contract(slots, back, 0, 0).astype(BF16)
        own = jnp.where(live, new_grad, own)
    outer = (left.astype(F32)[:, :, None] * right[:, None, :]).astype(BF16)
    outer = outer.reshape(n_rows, n_extra * feat)
    terms = jnp.zeros((n_rows, feat), F32)
    for number in range(n_extra):
        here = outer[:, number * feat : (number + 1) * feat]
        terms = terms + contract(sketch[number], here, 1, 0)
    back = exchange(terms.astype(BF16)).reshape(EXPERTS, n_expert // EXPERTS, block, feat)
    back = back[:, :, used : used + n_extra].astype(F32).sum(axis=1)
    back = back.reshape(EXPERTS, n_extra * feat)
    start = (lax.axis_index("expert") * q_dev) % EXPERTS
    found = lax.dynamic_slice_in_dim(back, start, q_dev, 0)
    return own.reshape(1, n_micro, tok_dev, feat), found[None]


def on_device(
    saved_inputs,
    top_grad,
    expert_ids,
    route_weights,
    example_ids,
    gate_weight,
    up_weight,
    down_weight,
    left_proj,
    right_proj,
):
    n_section = lax.axis_size("section")
    n_expert = lax.axis_size("expert")
    n_micro, tok_dev, feat = saved_inputs.shape[1:]
    top_k = expert_ids.shape[3]
    hidden = gate_weight.shape[1]
    tokens = n_micro * tok_dev
    sketch_dim = left_proj.shape[2]
    used = n_micro * CAP
    n_extra = sketch_dim * sketch_dim // feat
    block = -(-(used + n_extra) // 8) * 8
    n_rows = n_expert * block
    q_dev = n_micro * EXM * EXPERTS // n_expert
    share = -(-(n_expert * used // 2) // 8) * 8
    n_picks = n_expert * share

    def shape(*dims, dtype=BF16):
        return jax.ShapeDtypeStruct(dims, dtype)

    arrays = (
        expert_ids.transpose(0, 1, 3, 2),
        route_weights.transpose(0, 1, 3, 2),
        example_ids,
        saved_inputs,
        top_grad,
    )
    saved_send, top_send, slots = call(
        functools.partial(prepare, n_section, n_expert, block),
        (shape(n_rows, feat), shape(n_rows, feat), shape(n_rows, tokens)),
        arrays,
        HBM,
        [pltpu.VMEM(a.shape, a.dtype) for a in arrays] + [pltpu.SemaphoreType.DMA((5,))],
        60 << 20,
    )

    def exchange(rows):
        blocks = rows.reshape(n_expert, block, feat)
        blocks = lax.all_to_all(blocks, "expert", split_axis=0, concat_axis=0, tiled=True)
        return blocks.reshape(n_rows, feat)

    x_rows = exchange(saved_send)
    (fields,) = call(
        functools.partial(collect, block, used, 2 * top_k + 1),
        (shape(-(-(2 * top_k + 1) // 8) * 8, n_expert * tokens, dtype=F32),),
        (x_rows,),
    )
    around = [fields]
    for turn in range(1, n_section):
        pairs = [(i, (i - turn) % n_section) for i in range(n_section)]
        around.append(lax.ppermute(fields, "section", pairs))
    top_rows = exchange(top_send)
    tile = math.gcd(hidden, FORWARD)
    weight = gate_weight.shape
    left_map, right_map = left_proj.transpose(0, 2, 1), right_proj.transpose(0, 2, 1)
    to_gate, to_up, left = pl.pallas_call(
        forward,
        out_shape=(
            shape(n_rows, hidden, dtype=F32),
            shape(n_rows, hidden, dtype=F32),
            shape(n_rows, sketch_dim),
        ),
        in_specs=[VMEM, HBM, HBM, HBM],
        out_specs=(VMEM,) * 3,
        scratch_shapes=[
            pltpu.VMEM(weight, BF16),
            pltpu.VMEM(weight, BF16),
            pltpu.VMEM(left_map.shape, BF16),
            pltpu.SemaphoreType.DMA((1 + 2 * (hidden // tile),)),
        ],
        compiler_params=pltpu.CompilerParams(vmem_limit_bytes=58 << 20),
    )(x_rows, gate_weight, up_weight, left_map)
    comp, place, cols, sketch, over = call(
        functools.partial(
            plan, n_section, n_expert, n_micro, tok_dev, top_k, block, share, q_dev
        ),
        (
            shape(n_picks, n_rows),
            shape(n_rows, n_picks),
            shape(n_rows, LANES, dtype=F32),
            shape(n_extra, n_rows, n_rows),
            shape(8, LANES, dtype=F32),
        ),
        around,
        limit=(12 << 20) + 16 * n_rows * n_picks,
    )

    raw = (top_grad, gate_weight, up_weight, down_weight, left_proj, right_proj)

    def crowded(*_):
        return by_owners(
            block, used, n_extra, q_dev, raw, slots, x_rows, top_rows, cols, sketch
        )

    if n_expert > MOST_PERMUTES:
        return crowded()

    rows, part = None, None
    arrived = [top_rows]
    kept = (down_weight, to_gate, to_up, gate_weight, up_weight)
    for stage in range(n_section):
        last = stage == n_section - 1
        inputs = list(arrived) + ([place] if stage > 0 else [])
        specs = [VMEM] * len(inputs) + [VMEM if stage else HBM] * len(kept)
        inputs += list(kept) + [cols]
        if last:
            inputs += [rows, part, left, right_map, sketch]
            out = (shape(n_rows, feat),)
        else:
            inputs += [comp] + ([rows, part] if stage > 0 else [])
            out = tuple(shape(share, feat) for _ in range(n_expert))
            out += (shape(n_rows, feat), shape(n_rows, feat))
        specs += [VMEM] * (len(inputs) - len(specs))
        scratch = [
            pltpu.VMEM((n_rows, hidden), BF16),
            pltpu.VMEM((n_rows, hidden), BF16),
            pltpu.VMEM((n_rows, feat), BF16),
        ]
        if stage == 0:
            out += tuple(pltpu.VMEM(a.shape, a.dtype) for a in kept)
            scratch.append(pltpu.SemaphoreType.DMA((3 + 2 * HALVES,)))
        results = pl.pallas_call(
            functools.partial(
                layer, len(arrived), 0 if last else n_expert, stage > 0, stage, n_section, n_extra
            ),
            out_shape=out,
            in_specs=specs,
            out_specs=tuple(VMEM for _ in out),
            scratch_shapes=scratch,
            compiler_params=pltpu.CompilerParams(
                vmem_limit_bytes=(16 << 20) if stage else (38 << 20)
            ),
        )(*inputs)
        if last:
            back = exchange(results[0])
            break
        part, rows = results[n_expert : n_expert + 2]
        if stage == 0:
            kept = results[n_expert + 2 :]
        arrived = send_down(results[:n_expert], n_section - 1 - stage, n_expert)

    def direct(*_):
        return call(
            functools.partial(finish, n_expert, block, used, n_extra, q_dev),
            (
                shape(1, n_micro, tok_dev, feat),
                shape(1, q_dev, sketch_dim * sketch_dim, dtype=F32),
            ),
            (back, slots),
        )

    return lax.cond(over[0, 0] > share, crowded, direct)


def solution(mesh):
    placed = (
        P("section", None, "expert", None),
        P(None, "expert", None),
        P("section", None, "expert", None),
        P("section", None, "expert", None),
        P(None, "expert"),
        P("section", "expert", None),
        P("section", "expert", None),
        P("section", "expert", None),
        P("section", "expert", None),
        P("section", None, None),
    )
    return jax.shard_map(
        on_device,
        mesh=mesh,
        in_specs=placed,
        out_specs=(P("section", None, "expert", None), P("section", "expert", None)),
        check_vma=False,
    )
```

```python
import functools
import math

import jax
import jax.numpy as jnp
from jax import lax
from jax.experimental import pallas as pl
from jax.experimental.pallas import tpu as pltpu
from jax.sharding import PartitionSpec as P

EXPERTS = 8
EXM = 4
CAP = 3
LANES = 128
MOST_PERMUTES = 8
NARROW = (1536, 1)
WIDEN = (2048, 1)
FORWARD = 512
SKETCH = (2048, 1)

F32 = jnp.float32
BF16 = jnp.bfloat16
VMEM = pl.BlockSpec(memory_space=pltpu.VMEM)
HBM = pl.BlockSpec(memory_space=pltpu.HBM)


def contract(a, b, dim_a, dim_b):
    return lax.dot_general(a, b, (((dim_a,), (dim_b,)), ((), ())), preferred_element_type=F32)


def iota(shape, dim):
    return lax.broadcasted_iota(jnp.int32, shape, dim)


def ones_where(mask):
    return jnp.where(mask, 1.0, 0.0).astype(F32)


def partner(device, turn, amount):
    if amount & (amount - 1) == 0:
        return device ^ turn
    return (turn + 2 * amount - device) % amount


def size_of(arrays):
    return sum(a.dtype.itemsize * a.size for a in arrays)


def over_tiles(size, shape, body):
    tile, together = math.gcd(size, shape[0]), shape[1]

    def step(number, carry):
        body(pl.ds(pl.multiple_of(number * tile, tile), tile))
        return carry

    if size == tile:
        body(pl.ds(0, tile))
        return
    lax.fori_loop(0, size // tile, step, 0, unroll=math.gcd(size // tile, together))


def call(kernel, out_shape, inputs, spec=VMEM, scratch=(), limit=12 << 20):
    return pl.pallas_call(
        kernel,
        out_shape=out_shape,
        in_specs=[spec] * len(inputs),
        out_specs=tuple(VMEM for _ in out_shape),
        scratch_shapes=list(scratch),
        compiler_params=pltpu.CompilerParams(vmem_limit_bytes=limit),
    )(*inputs)


def copy_all(pairs, sems):
    copies = []
    for number, (source, target) in enumerate(pairs):
        copies.append(pltpu.make_async_copy(source, target, sems.at[number]))
        copies[-1].start()
    for copy in copies:
        copy.wait()


def names(fields, top_k, group):
    hit = fields[0:1, :] == group
    for k in range(1, top_k):
        hit = hit | (fields[k : k + 1, :] == group)
    return ones_where(hit)


def prepare(n_section, n_expert, block, ids_hbm, w_hbm, ex_hbm, x_hbm, top_hbm, *refs):
    send_ref, slots_ref = refs[:2]
    ids_ref, w_ref, ex_ref, x_ref, top_ref, sems = refs[2:]
    from_hbm = (ids_hbm, w_hbm, ex_hbm, x_hbm, top_hbm)
    copy_all(list(zip(from_hbm, (ids_ref, w_ref, ex_ref, x_ref, top_ref))), sems)
    n_micro, top_k, tok_dev = ids_ref.shape[1:]
    tokens = n_micro * tok_dev
    n_all = n_expert * tokens
    n_fields = 2 * top_k + 1
    feat = x_ref.shape[3]
    section, me = lax.axis_index("section"), lax.axis_index("expert")
    padded = -(-n_fields // 8) * 8
    local = jnp.zeros((padded, tokens), F32)
    packed = jnp.zeros((padded, n_all), F32)
    for m in range(n_micro):
        row = iota((padded, tok_dev), 0)
        example = ex_ref[m : m + 1, :] + m * EXM
        fields = jnp.where(row == 2 * top_k, example.astype(F32), 0.0)
        for k in range(top_k):
            fields = jnp.where(row == k, ids_ref[0, m, k : k + 1, :].astype(F32), fields)
            fields = jnp.where(row == top_k + k, w_ref[0, m, k : k + 1, :].astype(F32), fields)
        here = iota((tok_dev, tokens), 1) == m * tok_dev + iota((tok_dev, tokens), 0)
        local = local + contract(fields, ones_where(here), 1, 0)
        there = me * tokens + m * tok_dev + iota((tok_dev, n_all), 0)
        packed = packed + contract(fields, ones_where(iota((tok_dev, n_all), 1) == there), 1, 0)
    early, late = iota((tokens, tokens), 0), iota((tokens, tokens), 1)
    before = ones_where((early // tok_dev == late // tok_dev) & (early < late))

    def slots_in(height):
        at = (n_expert * height, tokens)
        group = (iota(at, 0) // (height * (n_expert // EXPERTS))).astype(F32)
        hit = names(local, top_k, group)
        position = contract(hit, before, 1, 0)
        slot = iota(at, 0) % block - CAP * (iota(at, 1) // tok_dev)
        fits = (hit > 0.5) & (slot >= 0) & (slot < CAP) & (position == slot.astype(F32))
        return ones_where(fits)

    slots_ref[...] = slots_in(block).astype(BF16)
    both = slots_in(2 * block)
    second = iota(both.shape, 0) % (2 * block) >= block
    for_saved = jnp.where(second, 0.0, both).astype(BF16)
    for_top = jnp.where(second & (section == n_section - 1), both, 0.0).astype(BF16)
    saved = jnp.concatenate([x_ref[0, m] for m in range(n_micro)], axis=0)
    top = jnp.concatenate([top_ref[m] for m in range(n_micro)], axis=0)
    send_ref[...] = (contract(for_saved, saved, 1, 0) + contract(for_top, top, 1, 0)).astype(BF16)
    spare_at = iota((2 * n_expert * block, n_all), 0) % (2 * block)
    for number, (at_row, lanes) in enumerate(field_places(n_fields, n_all, feat, n_micro * CAP)):
        field = jnp.broadcast_to(packed[number : number + 1, :], spare_at.shape)
        kept = send_ref[:, lanes].astype(F32)
        send_ref[:, lanes] = jnp.where(spare_at == at_row, field, kept).astype(BF16)


def field_places(n_fields, n_all, feat, first_row):
    per_row = feat // n_all
    for number in range(n_fields):
        at = number % per_row * n_all
        yield first_row + number // per_row, slice(at, at + n_all)


def collect(block, used, n_fields, x_ref, fields_ref):
    n_all = fields_ref.shape[1]
    rows, feat = x_ref.shape
    total = jnp.zeros(fields_ref.shape, F32)
    for number, (at_row, lanes) in enumerate(field_places(n_fields, n_all, feat, used)):
        spare = iota((rows, n_all), 0) % (2 * block) == at_row
        kept = jnp.where(spare, x_ref[:, lanes].astype(F32), 0.0)
        field = jnp.sum(kept, axis=0, keepdims=True)
        total = jnp.where(iota(fields_ref.shape, 0) == number, field, total)
    fields_ref[...] = total


def plan(
    n_section, n_expert, n_micro, tok_dev, top_k, block, share, q_dev, *refs
):
    around, refs = refs[:n_section], refs[n_section:]
    comp_ref, place_ref, cols_ref, sketch_ref, over_ref = refs
    n_all = around[0].shape[1]
    tokens = n_micro * tok_dev
    hsplit = n_expert // EXPERTS
    rows = n_expert * block
    section, me = lax.axis_index("section"), lax.axis_index("expert")
    mine, below, above = around[0][...], around[-1][...], around[1 % n_section][...]
    group = (me // hsplit).astype(F32)
    hit = names(mine, top_k, group)
    early, late = iota((n_all, n_all), 0), iota((n_all, n_all), 1)
    before = ones_where(early < late)
    near = ones_where((early // tok_dev == late // tok_dev) & (early < late))
    lane = iota((8, n_all), 1)
    count = contract(jnp.broadcast_to(hit, (8, n_all)), near, 1, 0)
    slot = (lane // tokens) * block + (lane // tok_dev) % n_micro * CAP
    slot = (slot.astype(F32) + count)[0:1, :]
    held = ones_where((iota((rows, n_all), 0).astype(F32) == slot) & (hit > 0.5))
    weight = jnp.zeros((1, n_all), F32)
    for k in range(top_k):
        weight = weight + jnp.where(
            mine[k : k + 1, :] == group, mine[top_k + k : top_k + k + 1, :], 0.0
        )
    first = ones_where((mine[0:1, :] == group) & (me % hsplit == 0))
    column = iota((rows, LANES), 1)
    weight_col = jnp.sum(held * weight, axis=1, keepdims=True)
    first_col = jnp.sum(held * first, axis=1, keepdims=True)
    cols_ref[...] = jnp.where(column == 0, weight_col, jnp.where(column == 1, first_col, 0.0))

    held_b = held.astype(BF16)
    peers = (partner(me, iota((n_expert, n_all), 0), n_expert) // hsplit).astype(F32)
    for other, to_row in ((below, True), (above, False)):
        both = names(other, top_k, peers) * hit
        position = contract(both, before, 1, 0)
        picks = []
        for turn in range(n_expert):
            chosen = position[turn : turn + 1, :] == iota((share, n_all), 0).astype(F32)
            picks.append(ones_where(chosen) * both[turn : turn + 1, :])
        picks = jnp.concatenate(picks, axis=0).astype(BF16)
        if to_row:
            comp_ref[...] = contract(picks, held_b, 1, 1).astype(BF16)
        else:
            place_ref[...] = contract(held_b, picks, 1, 1).astype(BF16)

    place = iota((rows, n_all), 0)
    target = (place // block) * q_dev
    local = me // hsplit
    inside = (local >= target % EXPERTS) & (local < target % EXPERTS + q_dev)
    example = mine[2 * top_k : 2 * top_k + 1, :]
    fits = inside & (example == (target // EXPERTS).astype(F32))
    for part_no in range(sketch_ref.shape[0]):
        at_row = place % block == n_micro * CAP + part_no
        terms = jnp.where(fits & at_row, weight, 0.0).astype(BF16)
        sketch_ref[part_no] = contract(terms, held_b, 1, 1).astype(BF16)

    expert = iota((EXPERTS, n_all), 0).astype(F32)
    most = jnp.zeros((1, 1), F32)
    upper = names(mine, top_k, expert)
    for turn in range(1, n_section + 1):
        lower, upper = upper, names(around[turn % n_section][...], top_k, expert)
        shared = jnp.max(contract(upper, lower, 1, 1), axis=(0, 1), keepdims=True)
        wraps = (section + turn) % n_section == 0
        most = jnp.maximum(most, jnp.where(wraps, 0.0, shared))
    over_ref[...] = jnp.broadcast_to(most, over_ref.shape)


def forward(
    block, both_ref, gate_hbm, up_hbm, down_hbm, left_hbm, right_hbm,
    to_gate_ref, to_up_ref, left_ref, top_ref, gate_ref, up_ref, down_ref, right_map, left_map, sems,
):
    n_rows, hidden = to_gate_ref.shape
    feat = top_ref.shape[1]
    tile = math.gcd(hidden, FORWARD)
    pairs = [(left_hbm, left_map)]
    for number in range(hidden // tile):
        part = pl.ds(number * tile, tile)
        pairs.append((gate_hbm.at[:, part, :], gate_ref.at[:, part, :]))
        pairs.append((up_hbm.at[:, part, :], up_ref.at[:, part, :]))
    pairs += [(down_hbm, down_ref), (right_hbm, right_map)]
    copies = [pltpu.make_async_copy(a, b, sems.at[i]) for i, (a, b) in enumerate(pairs)]
    for copy in copies:
        copy.start()
    both = both_ref[...].astype(F32).reshape(n_rows // block, 2 * block, feat)
    top_ref[...] = both[:, block:].reshape(n_rows, feat).astype(BF16)
    x = both[:, :block].reshape(n_rows, feat).astype(BF16)
    copies[0].wait()
    left = jnp.zeros(left_ref.shape, F32)
    for number in range(hidden // tile):
        part = slice(number * tile, (number + 1) * tile)
        copies[2 * number + 1].wait()
        gate = contract(x, gate_ref[0, part, :], 1, 1)
        copies[2 * number + 2].wait()
        up = contract(x, up_ref[0, part, :], 1, 1)
        sigmoid = jax.nn.sigmoid(gate)
        silu = gate * sigmoid
        to_up_ref[:, part] = silu
        to_gate_ref[:, part] = up * sigmoid * (1.0 + gate * (1.0 - sigmoid))
        left = left + contract((silu * up).astype(BF16), left_map[0, :, part], 1, 1)
    left_ref[...] = left.astype(BF16)
    for copy in copies[-2:]:
        copy.wait()


def layer(n_arrived, n_sent, n_before, stage, n_section, n_extra, *refs):
    refs = list(refs)
    take = lambda amount: [refs.pop(0) for _ in range(amount)]
    arrived = take(n_arrived)
    place = take(1)[0] if n_arrived > 1 else None
    down, to_gate, to_up, gate, up, cols = take(6)
    comp = take(1)[0] if n_sent else None
    rows_before, part_before = take(2) if n_before else (None, None)
    if not n_sent:
        left_ref, right_proj, sketch = take(3)
    sent = take(n_sent)
    part_ref, rows_ref = take(2) if n_sent else take(1) + [None]
    grad_gate, grad_up, rows_now = refs
    feat = rows_now.shape[1]
    live = lax.axis_index("section") == n_section - 1 - stage

    @pl.when(live)
    def _():
        if n_arrived > 1:
            pieces = jnp.concatenate([ref[...].astype(F32) for ref in arrived], axis=0)
            rows = contract(place[...], pieces.astype(BF16), 1, 0).astype(BF16)
        else:
            rows = arrived[0][...]
        rows_now[...] = rows
        def narrow(part):
            grad_hidden = contract(rows_now[...], down[0, part, :], 1, 1)
            grad_gate[:, part] = (grad_hidden * to_gate[:, part]).astype(BF16)
            grad_up[:, part] = (grad_hidden * to_up[:, part]).astype(BF16)

        over_tiles(grad_gate.shape[1], NARROW, narrow)

        def widen(part):
            total = contract(grad_gate[...], gate[0, :, part], 1, 0)
            total = total + contract(grad_up[...], up[0, :, part], 1, 0)
            kept = rows_now[:, part].astype(F32) * cols[:, 1:2]
            total = (total * cols[:, 0:1] + kept).astype(BF16)
            part_ref[:, part] = total
            if n_sent:
                chosen = contract(comp[...], total, 1, 0)
                share = chosen.shape[0] // n_sent
                for turn in range(n_sent):
                    sent[turn][:, part] = chosen[turn * share : (turn + 1) * share].astype(BF16)

        over_tiles(feat, WIDEN, widen)

    @pl.when(jnp.logical_not(live))
    def _():
        if n_before:
            rows_now[...] = rows_before[...]
            part_ref[...] = part_before[...]
        else:
            rows_now[...] = jnp.zeros(rows_now.shape, BF16)
            part_ref[...] = jnp.zeros(part_ref.shape, BF16)

    if n_sent:
        rows_ref[...] = rows_now[...]
        return
    right = contract(rows_now[...], right_proj[0], 1, 1)
    high = right.astype(BF16)
    low = (right - high.astype(F32)).astype(BF16)
    left = left_ref[...]
    size = left.shape[1]
    tile = math.gcd(feat, SKETCH[0])
    lane, axis = iota((size, tile), 1), iota((size, tile), 0)
    over_right = ones_where(axis == lane % size).astype(BF16)
    right = contract(high, over_right, 1, 0) + contract(low, over_right, 1, 0)
    for number in range(n_extra):

        def add_terms(part, number=number):
            over_left = ones_where(axis == (number * feat + part.start + lane) // size)
            outer = contract(left, over_left.astype(BF16), 1, 0) * right
            terms = contract(sketch[number], outer.astype(BF16), 1, 0)
            part_ref[:, part] = (part_ref[:, part].astype(F32) + terms).astype(BF16)

        over_tiles(feat, SKETCH, add_terms)


def finish(n_expert, block, used, n_extra, q_dev, back_ref, slots_ref, grad_ref, sketch_ref):
    me = lax.axis_index("expert")
    hsplit = n_expert // EXPERTS
    n_micro, tok_dev, feat = grad_ref.shape[1:]
    rows = n_expert * block
    start = (me * q_dev) % EXPERTS
    group = iota((q_dev, rows), 1) // (block * hsplit)
    owner = group == start + iota((q_dev, rows), 0)
    back = back_ref[...]
    total = contract(slots_ref[...], back, 0, 0)
    for m in range(n_micro):
        grad_ref[0, m] = total[m * tok_dev : (m + 1) * tok_dev].astype(BF16)
    for number in range(n_extra):
        at_row = iota((q_dev, rows), 1) % block == used + number
        picks = ones_where(owner & at_row).astype(BF16)
        sketch_ref[0, :, number * feat : (number + 1) * feat] = contract(picks, back, 1, 0)


def send_down(blocks, section, n_expert):
    window = 5
    quick, far = [0, n_expert // 4, 1], [n_expert // 2 + 1, n_expert // 2]
    late = [turn for turn in reversed(range(n_expert)) if turn not in quick + far]
    order = quick + far + late
    arrived = [None] * n_expert
    for place, turn in enumerate(order):
        pairs = [
            (section * n_expert + e, (section - 1) * n_expert + partner(e, turn, n_expert))
            for e in range(n_expert)
        ]
        block = blocks[turn]
        if place >= window:
            earlier = order[place - window]
            block, arrived[earlier] = lax.optimization_barrier((block, arrived[earlier]))
        arrived[turn] = lax.ppermute(block, ("section", "expert"), pairs)
    return arrived


def by_owners(block, used, n_extra, q_dev, arrays, slots, x_rows, top_rows, cols, sketch):
    top_grad, gate_weight, up_weight, down_weight, left_proj, right_proj = arrays
    n_section, n_expert = lax.axis_size("section"), lax.axis_size("expert")
    section = lax.axis_index("section")
    n_micro, tok_dev, feat = top_grad.shape
    tokens = n_micro * tok_dev
    n_rows = n_expert * block

    def exchange(rows):
        blocks = rows.reshape(n_expert, block, feat)
        blocks = lax.all_to_all(blocks, "expert", split_axis=0, concat_axis=0, tiled=True)
        return blocks.reshape(n_rows, feat)

    gate, up, down = gate_weight[0], up_weight[0], down_weight[0]
    pre_gate = contract(x_rows, gate, 1, 1)
    pre_up = contract(x_rows, up, 1, 1)
    sigmoid = jax.nn.sigmoid(pre_gate)
    to_up = pre_gate * sigmoid
    to_gate = pre_up * sigmoid * (1.0 + pre_gate * (1.0 - sigmoid))
    left = contract((to_up * pre_up).astype(BF16), left_proj[0], 1, 0).astype(BF16)
    size = left.shape[1]
    rows = top_rows
    right = jnp.zeros((n_rows, size), F32)
    own = jnp.zeros((tokens, feat), BF16)
    for stage in range(n_section):
        live = section == n_section - 1 - stage
        if stage > 0:
            hop = [(n_section - stage, n_section - 1 - stage)]
            out_grad = lax.ppermute(new_grad, "section", hop)
            rows = exchange(contract(slots, out_grad, 1, 0).astype(BF16))
        grad_hidden = contract(rows, down, 1, 1)
        part = contract((grad_hidden * to_gate).astype(BF16), gate, 1, 0)
        part = part + contract((grad_hidden * to_up).astype(BF16), up, 1, 0)
        part = part * cols[:, 0:1] + rows.astype(F32) * cols[:, 1:2]
        right = right + jnp.where(live, contract(rows, right_proj[0], 1, 0), 0.0)
        back = exchange(part.astype(BF16))
        new_grad = contract(slots, back, 0, 0).astype(BF16)
        own = jnp.where(live, new_grad, own)
    outer = (left.astype(F32)[:, :, None] * right[:, None, :]).astype(BF16)
    outer = outer.reshape(n_rows, n_extra * feat)
    terms = jnp.zeros((n_rows, feat), F32)
    for number in range(n_extra):
        here = outer[:, number * feat : (number + 1) * feat]
        terms = terms + contract(sketch[number], here, 1, 0)
    back = exchange(terms.astype(BF16)).reshape(EXPERTS, n_expert // EXPERTS, block, feat)
    back = back[:, :, used : used + n_extra].astype(F32).sum(axis=1)
    back = back.reshape(EXPERTS, n_extra * feat)
    start = (lax.axis_index("expert") * q_dev) % EXPERTS
    found = lax.dynamic_slice_in_dim(back, start, q_dev, 0)
    return own.reshape(1, n_micro, tok_dev, feat), found[None]


def on_device(
    saved_inputs,
    top_grad,
    expert_ids,
    route_weights,
    example_ids,
    gate_weight,
    up_weight,
    down_weight,
    left_proj,
    right_proj,
):
    n_section = lax.axis_size("section")
    n_expert = lax.axis_size("expert")
    n_micro, tok_dev, feat = saved_inputs.shape[1:]
    top_k = expert_ids.shape[3]
    hidden = gate_weight.shape[1]
    tokens = n_micro * tok_dev
    sketch_dim = left_proj.shape[2]
    used = n_micro * CAP
    n_extra = sketch_dim * sketch_dim // feat
    block = -(-(used + n_extra) // 8) * 8
    n_rows = n_expert * block
    q_dev = n_micro * EXM * EXPERTS // n_expert
    share = -(-(n_expert * used // 2) // 8) * 8
    n_picks = n_expert * share

    def shape(*dims, dtype=BF16):
        return jax.ShapeDtypeStruct(dims, dtype)

    arrays = (
        expert_ids.transpose(0, 1, 3, 2),
        route_weights.transpose(0, 1, 3, 2),
        example_ids,
        saved_inputs,
        top_grad,
    )
    send, slots = call(
        functools.partial(prepare, n_section, n_expert, block),
        (shape(2 * n_rows, feat), shape(n_rows, tokens)),
        arrays,
        HBM,
        [pltpu.VMEM(a.shape, a.dtype) for a in arrays] + [pltpu.SemaphoreType.DMA((5,))],
        60 << 20,
    )

    def exchange(rows):
        blocks = rows.reshape(n_expert, rows.shape[0] // n_expert, feat)
        blocks = lax.all_to_all(blocks, "expert", split_axis=0, concat_axis=0, tiled=True)
        return blocks.reshape(rows.shape)

    both = exchange(send)
    (fields,) = call(
        functools.partial(collect, block, used, 2 * top_k + 1),
        (shape(-(-(2 * top_k + 1) // 8) * 8, n_expert * tokens, dtype=F32),),
        (both,),
    )
    around = [fields]
    for turn in range(1, n_section):
        pairs = [(i, (i - turn) % n_section) for i in range(n_section)]
        around.append(lax.ppermute(fields, "section", pairs))
    tile = math.gcd(hidden, FORWARD)
    left_map, right_map = left_proj.transpose(0, 2, 1), right_proj.transpose(0, 2, 1)
    stored = (gate_weight, up_weight, down_weight, left_map, right_map)
    to_gate, to_up, left, top_rows, gate, up, down, right_map = pl.pallas_call(
        functools.partial(forward, block),
        out_shape=(
            pltpu.VMEM((n_rows, hidden), F32),
            pltpu.VMEM((n_rows, hidden), F32),
            shape(n_rows, sketch_dim),
            shape(n_rows, feat),
        )
        + tuple(pltpu.VMEM(stored[i].shape, BF16) for i in (0, 1, 2, 4)),
        in_specs=[VMEM] + [HBM] * len(stored),
        out_specs=(VMEM,) * 8,
        scratch_shapes=[
            pltpu.VMEM(left_map.shape, BF16),
            pltpu.SemaphoreType.DMA((3 + 2 * (hidden // tile),)),
        ],
        compiler_params=pltpu.CompilerParams(vmem_limit_bytes=38 << 20),
    )(both, *stored)
    comp, place, cols, sketch, over = call(
        functools.partial(
            plan, n_section, n_expert, n_micro, tok_dev, top_k, block, share, q_dev
        ),
        (
            shape(n_picks, n_rows),
            shape(n_rows, n_picks),
            shape(n_rows, LANES, dtype=F32),
            shape(n_extra, n_rows, n_rows),
            shape(8, LANES, dtype=F32),
        ),
        around,
        limit=(12 << 20) + 16 * n_rows * n_picks,
    )

    raw = (top_grad, gate_weight, up_weight, down_weight, left_proj, right_proj)

    def crowded(*_):
        x_rows = both.reshape(n_expert, 2 * block, feat)[:, :block].reshape(n_rows, feat)
        return by_owners(
            block, used, n_extra, q_dev, raw, slots, x_rows, top_rows, cols, sketch
        )

    if n_expert > MOST_PERMUTES:
        return crowded()

    rows, part = None, None
    arrived = [top_rows]
    for stage in range(n_section):
        last = stage == n_section - 1
        inputs = list(arrived) + ([place] if stage > 0 else [])
        inputs += [down, to_gate, to_up, gate, up, cols]
        if last:
            inputs += [rows, part, left, right_map, sketch]
            out = (shape(n_rows, feat),)
        else:
            inputs += [comp] + ([rows, part] if stage > 0 else [])
            out = tuple(shape(share, feat) for _ in range(n_expert))
            out += (shape(n_rows, feat), shape(n_rows, feat))
        results = call(
            functools.partial(
                layer, len(arrived), 0 if last else n_expert, stage > 0, stage, n_section, n_extra
            ),
            out,
            inputs,
            scratch=[
                pltpu.VMEM((n_rows, hidden), BF16),
                pltpu.VMEM((n_rows, hidden), BF16),
                pltpu.VMEM((n_rows, feat), BF16),
            ],
            limit=16 << 20,
        )
        if last:
            back = exchange(results[0])
            break
        part, rows = results[n_expert:]
        arrived = send_down(results[:n_expert], n_section - 1 - stage, n_expert)

    def direct(*_):
        return call(
            functools.partial(finish, n_expert, block, used, n_extra, q_dev),
            (
                shape(1, n_micro, tok_dev, feat),
                shape(1, q_dev, sketch_dim * sketch_dim, dtype=F32),
            ),
            (back, slots),
        )

    return lax.cond(over[0, 0] > share, crowded, direct)


def solution(mesh):
    placed = (
        P("section", None, "expert", None),
        P(None, "expert", None),
        P("section", None, "expert", None),
        P("section", None, "expert", None),
        P(None, "expert"),
        P("section", "expert", None),
        P("section", "expert", None),
        P("section", "expert", None),
        P("section", "expert", None),
        P("section", None, None),
    )
    return jax.shard_map(
        on_device,
        mesh=mesh,
        in_specs=placed,
        out_specs=(P("section", None, "expert", None), P("section", "expert", None)),
        check_vma=False,
    )
```

```python
import functools
import math

import jax
import jax.numpy as jnp
from jax import lax
from jax.experimental import pallas as pl
from jax.experimental.pallas import tpu as pltpu
from jax.sharding import PartitionSpec as P

EXPERTS = 8
EXM = 4
CAP = 3
LANES = 128
MOST_PERMUTES = 8
NARROW = (1536, 1)
WIDEN = (2048, 1)
FORWARD = 512

F32 = jnp.float32
BF16 = jnp.bfloat16
VMEM = pl.BlockSpec(memory_space=pltpu.VMEM)
HBM = pl.BlockSpec(memory_space=pltpu.HBM)


def contract(a, b, dim_a, dim_b):
    return lax.dot_general(a, b, (((dim_a,), (dim_b,)), ((), ())), preferred_element_type=F32)


def iota(shape, dim):
    return lax.broadcasted_iota(jnp.int32, shape, dim)


def ones_where(mask):
    return jnp.where(mask, 1.0, 0.0).astype(F32)


def partner(device, turn, amount):
    if amount & (amount - 1) == 0:
        return device ^ turn
    return (turn + 2 * amount - device) % amount


def size_of(arrays):
    return sum(a.dtype.itemsize * a.size for a in arrays)


def over_tiles(size, shape, body):
    tile, together = math.gcd(size, shape[0]), shape[1]

    def step(number, carry):
        body(pl.ds(pl.multiple_of(number * tile, tile), tile))
        return carry

    if size == tile:
        body(pl.ds(0, tile))
        return
    lax.fori_loop(0, size // tile, step, 0, unroll=math.gcd(size // tile, together))


def call(kernel, out_shape, inputs, spec=VMEM, scratch=(), limit=12 << 20):
    return pl.pallas_call(
        kernel,
        out_shape=out_shape,
        in_specs=[spec] * len(inputs),
        out_specs=tuple(VMEM for _ in out_shape),
        scratch_shapes=list(scratch),
        compiler_params=pltpu.CompilerParams(vmem_limit_bytes=limit),
    )(*inputs)


def copy_all(pairs, sems):
    copies = []
    for number, (source, target) in enumerate(pairs):
        copies.append(pltpu.make_async_copy(source, target, sems.at[number]))
        copies[-1].start()
    for copy in copies:
        copy.wait()


def names(fields, top_k, group):
    hit = fields[0:1, :] == group
    for k in range(1, top_k):
        hit = hit | (fields[k : k + 1, :] == group)
    return ones_where(hit)


def prepare(n_section, n_expert, block, ids_hbm, w_hbm, ex_hbm, x_hbm, top_hbm, *refs):
    send_ref, slots_ref = refs[:2]
    ids_ref, w_ref, ex_ref, x_ref, top_ref, sems = refs[2:]
    from_hbm = (ids_hbm, w_hbm, ex_hbm, x_hbm, top_hbm)
    copy_all(list(zip(from_hbm, (ids_ref, w_ref, ex_ref, x_ref, top_ref))), sems)
    n_micro, top_k, tok_dev = ids_ref.shape[1:]
    tokens = n_micro * tok_dev
    n_all = n_expert * tokens
    n_fields = 2 * top_k + 1
    feat = x_ref.shape[3]
    section, me = lax.axis_index("section"), lax.axis_index("expert")
    padded = -(-n_fields // 8) * 8
    local = jnp.zeros((padded, tokens), F32)
    packed = jnp.zeros((padded, n_all), F32)
    for m in range(n_micro):
        row = iota((padded, tok_dev), 0)
        example = ex_ref[m : m + 1, :] + m * EXM
        fields = jnp.where(row == 2 * top_k, example.astype(F32), 0.0)
        for k in range(top_k):
            fields = jnp.where(row == k, ids_ref[0, m, k : k + 1, :].astype(F32), fields)
            fields = jnp.where(row == top_k + k, w_ref[0, m, k : k + 1, :].astype(F32), fields)
        here = iota((tok_dev, tokens), 1) == m * tok_dev + iota((tok_dev, tokens), 0)
        local = local + contract(fields, ones_where(here), 1, 0)
        there = me * tokens + m * tok_dev + iota((tok_dev, n_all), 0)
        packed = packed + contract(fields, ones_where(iota((tok_dev, n_all), 1) == there), 1, 0)
    early, late = iota((tokens, tokens), 0), iota((tokens, tokens), 1)
    before = ones_where((early // tok_dev == late // tok_dev) & (early < late))

    def slots_in(height):
        at = (n_expert * height, tokens)
        group = (iota(at, 0) // (height * (n_expert // EXPERTS))).astype(F32)
        hit = names(local, top_k, group)
        position = contract(hit, before, 1, 0)
        slot = iota(at, 0) % block - CAP * (iota(at, 1) // tok_dev)
        fits = (hit > 0.5) & (slot >= 0) & (slot < CAP) & (position == slot.astype(F32))
        return ones_where(fits)

    slots_ref[...] = slots_in(block).astype(BF16)
    both = slots_in(2 * block)
    second = iota(both.shape, 0) % (2 * block) >= block
    for_saved = jnp.where(second, 0.0, both).astype(BF16)
    for_top = jnp.where(second & (section == n_section - 1), both, 0.0).astype(BF16)
    saved = jnp.concatenate([x_ref[0, m] for m in range(n_micro)], axis=0)
    top = jnp.concatenate([top_ref[m] for m in range(n_micro)], axis=0)
    send_ref[...] = (contract(for_saved, saved, 1, 0) + contract(for_top, top, 1, 0)).astype(BF16)
    spare_at = iota((2 * n_expert * block, n_all), 0) % (2 * block)
    for number, (at_row, lanes) in enumerate(field_places(n_fields, n_all, feat, n_micro * CAP)):
        field = jnp.broadcast_to(packed[number : number + 1, :], spare_at.shape)
        kept = send_ref[:, lanes].astype(F32)
        send_ref[:, lanes] = jnp.where(spare_at == at_row, field, kept).astype(BF16)


def field_places(n_fields, n_all, feat, first_row):
    per_row = feat // n_all
    for number in range(n_fields):
        at = number % per_row * n_all
        yield first_row + number // per_row, slice(at, at + n_all)


def collect(block, used, n_fields, x_ref, fields_ref):
    n_all = fields_ref.shape[1]
    rows, feat = x_ref.shape
    total = jnp.zeros(fields_ref.shape, F32)
    for number, (at_row, lanes) in enumerate(field_places(n_fields, n_all, feat, used)):
        spare = iota((rows, n_all), 0) % (2 * block) == at_row
        kept = jnp.where(spare, x_ref[:, lanes].astype(F32), 0.0)
        field = jnp.sum(kept, axis=0, keepdims=True)
        total = jnp.where(iota(fields_ref.shape, 0) == number, field, total)
    fields_ref[...] = total


def plan(
    n_section, n_expert, n_micro, tok_dev, top_k, block, share, q_dev, *refs
):
    around, refs = refs[:n_section], refs[n_section:]
    comp_ref, place_ref, cols_ref, sketch_ref, over_ref = refs
    n_all = around[0].shape[1]
    tokens = n_micro * tok_dev
    hsplit = n_expert // EXPERTS
    rows = n_expert * block
    section, me = lax.axis_index("section"), lax.axis_index("expert")
    mine, below, above = around[0][...], around[-1][...], around[1 % n_section][...]
    group = (me // hsplit).astype(F32)
    hit = names(mine, top_k, group)
    early, late = iota((n_all, n_all), 0), iota((n_all, n_all), 1)
    before = ones_where(early < late)
    near = ones_where((early // tok_dev == late // tok_dev) & (early < late))
    lane = iota((8, n_all), 1)
    count = contract(jnp.broadcast_to(hit, (8, n_all)), near, 1, 0)
    slot = (lane // tokens) * block + (lane // tok_dev) % n_micro * CAP
    slot = (slot.astype(F32) + count)[0:1, :]
    held = ones_where((iota((rows, n_all), 0).astype(F32) == slot) & (hit > 0.5))
    weight = jnp.zeros((1, n_all), F32)
    for k in range(top_k):
        weight = weight + jnp.where(
            mine[k : k + 1, :] == group, mine[top_k + k : top_k + k + 1, :], 0.0
        )
    first = ones_where((mine[0:1, :] == group) & (me % hsplit == 0))
    column = iota((rows, LANES), 1)
    weight_col = jnp.sum(held * weight, axis=1, keepdims=True)
    first_col = jnp.sum(held * first, axis=1, keepdims=True)
    cols_ref[...] = jnp.where(column == 0, weight_col, jnp.where(column == 1, first_col, 0.0))

    held_b = held.astype(BF16)
    peers = (partner(me, iota((n_expert, n_all), 0), n_expert) // hsplit).astype(F32)
    for other, to_row in ((below, True), (above, False)):
        both = names(other, top_k, peers) * hit
        position = contract(both, before, 1, 0)
        picks = []
        for turn in range(n_expert):
            chosen = position[turn : turn + 1, :] == iota((share, n_all), 0).astype(F32)
            picks.append(ones_where(chosen) * both[turn : turn + 1, :])
        picks = jnp.concatenate(picks, axis=0).astype(BF16)
        if to_row:
            comp_ref[...] = contract(picks, held_b, 1, 1).astype(BF16)
        else:
            place_ref[...] = contract(held_b, picks, 1, 1).astype(BF16)

    place = iota((rows, n_all), 0)
    target = (place // block) * q_dev
    local = me // hsplit
    inside = (local >= target % EXPERTS) & (local < target % EXPERTS + q_dev)
    example = mine[2 * top_k : 2 * top_k + 1, :]
    fits = inside & (example == (target // EXPERTS).astype(F32))
    for part_no in range(sketch_ref.shape[0]):
        at_row = place % block == n_micro * CAP + part_no
        terms = jnp.where(fits & at_row, weight, 0.0).astype(BF16)
        sketch_ref[part_no] = contract(terms, held_b, 1, 1).astype(BF16)

    expert = iota((EXPERTS, n_all), 0).astype(F32)
    most = jnp.zeros((1, 1), F32)
    upper = names(mine, top_k, expert)
    for turn in range(1, n_section + 1):
        lower, upper = upper, names(around[turn % n_section][...], top_k, expert)
        shared = jnp.max(contract(upper, lower, 1, 1), axis=(0, 1), keepdims=True)
        wraps = (section + turn) % n_section == 0
        most = jnp.maximum(most, jnp.where(wraps, 0.0, shared))
    over_ref[...] = jnp.broadcast_to(most, over_ref.shape)


def forward(
    block, both_ref, gate_hbm, up_hbm, down_hbm, left_hbm, right_hbm,
    to_gate_ref, to_up_ref, left_ref, top_ref, gate_ref, up_ref, down_ref, right_map, left_map, sems,
):
    n_rows, hidden = to_gate_ref.shape
    feat = top_ref.shape[1]
    tile = math.gcd(hidden, FORWARD)
    pairs = [(left_hbm, left_map)]
    for number in range(hidden // tile):
        part = pl.ds(number * tile, tile)
        pairs.append((gate_hbm.at[:, part, :], gate_ref.at[:, part, :]))
        pairs.append((up_hbm.at[:, part, :], up_ref.at[:, part, :]))
    pairs += [(down_hbm, down_ref), (right_hbm, right_map)]
    copies = [pltpu.make_async_copy(a, b, sems.at[i]) for i, (a, b) in enumerate(pairs)]
    for copy in copies:
        copy.start()
    both = both_ref[...].astype(F32).reshape(n_rows // block, 2 * block, feat)
    top_ref[...] = both[:, block:].reshape(n_rows, feat).astype(BF16)
    x = both[:, :block].reshape(n_rows, feat).astype(BF16)
    copies[0].wait()
    size = left_map.shape[1]
    left = jnp.zeros((n_rows, size), F32)
    for number in range(hidden // tile):
        part = slice(number * tile, (number + 1) * tile)
        copies[2 * number + 1].wait()
        gate = contract(x, gate_ref[0, part, :], 1, 1)
        copies[2 * number + 2].wait()
        up = contract(x, up_ref[0, part, :], 1, 1)
        sigmoid = jax.nn.sigmoid(gate)
        silu = gate * sigmoid
        to_up_ref[:, part] = silu
        to_gate_ref[:, part] = up * sigmoid * (1.0 + gate * (1.0 - sigmoid))
        left = left + contract((silu * up).astype(BF16), left_map[0, :, part], 1, 1)
    left = left.astype(BF16)
    for at in range(0, left_ref.shape[1], feat):
        lane, axis = at + iota((size, feat), 1), iota((size, feat), 0)
        over_left = ones_where(axis == lane // size).astype(BF16)
        left_ref[:, at : at + feat] = contract(left, over_left, 1, 0).astype(BF16)
    for copy in copies[-2:]:
        copy.wait()


def layer(n_arrived, n_sent, n_before, stage, n_section, n_extra, *refs):
    refs = list(refs)
    take = lambda amount: [refs.pop(0) for _ in range(amount)]
    arrived = take(n_arrived)
    place = take(1)[0] if n_arrived > 1 else None
    down, to_gate, to_up, gate, up, cols = take(6)
    comp = take(1)[0] if n_sent else None
    rows_before, part_before = take(2) if n_before else (None, None)
    if not n_sent:
        left_ref, right_proj, sketch = take(3)
    sent = take(n_sent)
    part_ref, rows_ref = take(2) if n_sent else take(1) + [None]
    grad_gate, grad_up, rows_now = refs
    feat = rows_now.shape[1]
    live = lax.axis_index("section") == n_section - 1 - stage

    @pl.when(live)
    def _():
        if n_arrived > 1:
            pieces = jnp.concatenate([ref[...].astype(F32) for ref in arrived], axis=0)
            rows = contract(place[...], pieces.astype(BF16), 1, 0).astype(BF16)
        else:
            rows = arrived[0][...]
        rows_now[...] = rows
        def narrow(part):
            grad_hidden = contract(rows_now[...], down[0, part, :], 1, 1)
            grad_gate[:, part] = (grad_hidden * to_gate[:, part]).astype(BF16)
            grad_up[:, part] = (grad_hidden * to_up[:, part]).astype(BF16)

        over_tiles(grad_gate.shape[1], NARROW, narrow)

        def widen(part):
            total = contract(grad_gate[...], gate[0, :, part], 1, 0)
            total = total + contract(grad_up[...], up[0, :, part], 1, 0)
            kept = rows_now[:, part].astype(F32) * cols[:, 1:2]
            total = (total * cols[:, 0:1] + kept).astype(BF16)
            part_ref[:, part] = total
            if n_sent:
                chosen = contract(comp[...], total, 1, 0)
                share = chosen.shape[0] // n_sent
                for turn in range(n_sent):
                    sent[turn][:, part] = chosen[turn * share : (turn + 1) * share].astype(BF16)

        over_tiles(feat, WIDEN, widen)

    @pl.when(jnp.logical_not(live))
    def _():
        if n_before:
            rows_now[...] = rows_before[...]
            part_ref[...] = part_before[...]
        else:
            rows_now[...] = jnp.zeros(rows_now.shape, BF16)
            part_ref[...] = jnp.zeros(part_ref.shape, BF16)

    if n_sent:
        rows_ref[...] = rows_now[...]
        return
    right = contract(rows_now[...], right_proj[0], 1, 1)
    high = right.astype(BF16)
    low = (right - high.astype(F32)).astype(BF16)
    size = right.shape[1]
    width = math.gcd(feat, 2 * LANES)
    over_right = iota((size, width), 0) == iota((size, width), 1) % size
    over_right = ones_where(over_right).astype(BF16)
    right = contract(high, over_right, 1, 0) + contract(low, over_right, 1, 0)
    right = jnp.concatenate([right] * (feat // width), axis=1)
    for number in range(n_extra):
        part = slice(number * feat, (number + 1) * feat)
        outer = left_ref[:, part].astype(F32) * right
        terms = contract(sketch[number], outer.astype(BF16), 1, 0)
        part_ref[...] = (part_ref[...].astype(F32) + terms).astype(BF16)


def finish(n_expert, block, used, n_extra, q_dev, back_ref, slots_ref, grad_ref, sketch_ref):
    me = lax.axis_index("expert")
    hsplit = n_expert // EXPERTS
    n_micro, tok_dev, feat = grad_ref.shape[1:]
    rows = n_expert * block
    start = (me * q_dev) % EXPERTS
    group = iota((q_dev, rows), 1) // (block * hsplit)
    owner = group == start + iota((q_dev, rows), 0)
    back = back_ref[...]
    total = contract(slots_ref[...], back, 0, 0)
    for m in range(n_micro):
        grad_ref[0, m] = total[m * tok_dev : (m + 1) * tok_dev].astype(BF16)
    for number in range(n_extra):
        at_row = iota((q_dev, rows), 1) % block == used + number
        picks = ones_where(owner & at_row).astype(BF16)
        sketch_ref[0, :, number * feat : (number + 1) * feat] = contract(picks, back, 1, 0)


def send_down(blocks, section, n_expert):
    window = 5
    quick, far = [0, n_expert // 4, 1], [n_expert // 2 + 1, n_expert // 2]
    late = [turn for turn in reversed(range(n_expert)) if turn not in quick + far]
    order = quick + far + late
    arrived = [None] * n_expert
    for place, turn in enumerate(order):
        pairs = [
            (section * n_expert + e, (section - 1) * n_expert + partner(e, turn, n_expert))
            for e in range(n_expert)
        ]
        block = blocks[turn]
        if place >= window:
            earlier = order[place - window]
            block, arrived[earlier] = lax.optimization_barrier((block, arrived[earlier]))
        arrived[turn] = lax.ppermute(block, ("section", "expert"), pairs)
    return arrived


def by_owners(block, used, n_extra, q_dev, arrays, slots, x_rows, top_rows, cols, sketch):
    top_grad, gate_weight, up_weight, down_weight, left_proj, right_proj = arrays
    n_section, n_expert = lax.axis_size("section"), lax.axis_size("expert")
    section = lax.axis_index("section")
    n_micro, tok_dev, feat = top_grad.shape
    tokens = n_micro * tok_dev
    n_rows = n_expert * block

    def exchange(rows):
        blocks = rows.reshape(n_expert, block, feat)
        blocks = lax.all_to_all(blocks, "expert", split_axis=0, concat_axis=0, tiled=True)
        return blocks.reshape(n_rows, feat)

    gate, up, down = gate_weight[0], up_weight[0], down_weight[0]
    pre_gate = contract(x_rows, gate, 1, 1)
    pre_up = contract(x_rows, up, 1, 1)
    sigmoid = jax.nn.sigmoid(pre_gate)
    to_up = pre_gate * sigmoid
    to_gate = pre_up * sigmoid * (1.0 + pre_gate * (1.0 - sigmoid))
    left = contract((to_up * pre_up).astype(BF16), left_proj[0], 1, 0).astype(BF16)
    size = left.shape[1]
    rows = top_rows
    right = jnp.zeros((n_rows, size), F32)
    own = jnp.zeros((tokens, feat), BF16)
    for stage in range(n_section):
        live = section == n_section - 1 - stage
        if stage > 0:
            hop = [(n_section - stage, n_section - 1 - stage)]
            out_grad = lax.ppermute(new_grad, "section", hop)
            rows = exchange(contract(slots, out_grad, 1, 0).astype(BF16))
        grad_hidden = contract(rows, down, 1, 1)
        part = contract((grad_hidden * to_gate).astype(BF16), gate, 1, 0)
        part = part + contract((grad_hidden * to_up).astype(BF16), up, 1, 0)
        part = part * cols[:, 0:1] + rows.astype(F32) * cols[:, 1:2]
        right = right + jnp.where(live, contract(rows, right_proj[0], 1, 0), 0.0)
        back = exchange(part.astype(BF16))
        new_grad = contract(slots, back, 0, 0).astype(BF16)
        own = jnp.where(live, new_grad, own)
    outer = (left.astype(F32)[:, :, None] * right[:, None, :]).astype(BF16)
    outer = outer.reshape(n_rows, n_extra * feat)
    terms = jnp.zeros((n_rows, feat), F32)
    for number in range(n_extra):
        here = outer[:, number * feat : (number + 1) * feat]
        terms = terms + contract(sketch[number], here, 1, 0)
    back = exchange(terms.astype(BF16)).reshape(EXPERTS, n_expert // EXPERTS, block, feat)
    back = back[:, :, used : used + n_extra].astype(F32).sum(axis=1)
    back = back.reshape(EXPERTS, n_extra * feat)
    start = (lax.axis_index("expert") * q_dev) % EXPERTS
    found = lax.dynamic_slice_in_dim(back, start, q_dev, 0)
    return own.reshape(1, n_micro, tok_dev, feat), found[None]


def on_device(
    saved_inputs,
    top_grad,
    expert_ids,
    route_weights,
    example_ids,
    gate_weight,
    up_weight,
    down_weight,
    left_proj,
    right_proj,
):
    n_section = lax.axis_size("section")
    n_expert = lax.axis_size("expert")
    n_micro, tok_dev, feat = saved_inputs.shape[1:]
    top_k = expert_ids.shape[3]
    hidden = gate_weight.shape[1]
    tokens = n_micro * tok_dev
    sketch_dim = left_proj.shape[2]
    used = n_micro * CAP
    n_extra = sketch_dim * sketch_dim // feat
    block = -(-(used + n_extra) // 8) * 8
    n_rows = n_expert * block
    q_dev = n_micro * EXM * EXPERTS // n_expert
    share = -(-(n_expert * used // 2) // 8) * 8
    n_picks = n_expert * share

    def shape(*dims, dtype=BF16):
        return jax.ShapeDtypeStruct(dims, dtype)

    arrays = (
        expert_ids.transpose(0, 1, 3, 2),
        route_weights.transpose(0, 1, 3, 2),
        example_ids,
        saved_inputs,
        top_grad,
    )
    send, slots = call(
        functools.partial(prepare, n_section, n_expert, block),
        (pltpu.VMEM((2 * n_rows, feat), BF16), shape(n_rows, tokens)),
        arrays,
        HBM,
        [pltpu.VMEM(a.shape, a.dtype) for a in arrays] + [pltpu.SemaphoreType.DMA((5,))],
        58 << 20,
    )

    def exchange(rows):
        blocks = rows.reshape(n_expert, rows.shape[0] // n_expert, feat)
        blocks = lax.all_to_all(blocks, "expert", split_axis=0, concat_axis=0, tiled=True)
        return blocks.reshape(rows.shape)

    both = exchange(send)
    (fields,) = call(
        functools.partial(collect, block, used, 2 * top_k + 1),
        (shape(-(-(2 * top_k + 1) // 8) * 8, n_expert * tokens, dtype=F32),),
        (both,),
    )
    around = [fields]
    for turn in range(1, n_section):
        pairs = [(i, (i - turn) % n_section) for i in range(n_section)]
        around.append(lax.ppermute(fields, "section", pairs))
    tile = math.gcd(hidden, FORWARD)
    left_map, right_map = left_proj.transpose(0, 2, 1), right_proj.transpose(0, 2, 1)
    stored = (gate_weight, up_weight, down_weight, left_map, right_map)
    to_gate, to_up, left, top_rows, gate, up, down, right_map = pl.pallas_call(
        functools.partial(forward, block),
        out_shape=(
            pltpu.VMEM((n_rows, hidden), F32),
            pltpu.VMEM((n_rows, hidden), F32),
            pltpu.VMEM((n_rows, n_extra * feat), BF16),
            shape(n_rows, feat),
        )
        + tuple(pltpu.VMEM(stored[i].shape, BF16) for i in (0, 1, 2, 4)),
        in_specs=[VMEM] + [HBM] * len(stored),
        out_specs=(VMEM,) * 8,
        scratch_shapes=[
            pltpu.VMEM(left_map.shape, BF16),
            pltpu.SemaphoreType.DMA((3 + 2 * (hidden // tile),)),
        ],
        compiler_params=pltpu.CompilerParams(vmem_limit_bytes=38 << 20),
    )(both, *stored)
    comp, place, cols, sketch, over = call(
        functools.partial(
            plan, n_section, n_expert, n_micro, tok_dev, top_k, block, share, q_dev
        ),
        (
            shape(n_picks, n_rows),
            shape(n_rows, n_picks),
            shape(n_rows, LANES, dtype=F32),
            shape(n_extra, n_rows, n_rows),
            shape(8, LANES, dtype=F32),
        ),
        around,
        limit=(12 << 20) + 16 * n_rows * n_picks,
    )

    raw = (top_grad, gate_weight, up_weight, down_weight, left_proj, right_proj)

    def crowded(*_):
        x_rows = both.reshape(n_expert, 2 * block, feat)[:, :block].reshape(n_rows, feat)
        return by_owners(
            block, used, n_extra, q_dev, raw, slots, x_rows, top_rows, cols, sketch
        )

    if n_expert > MOST_PERMUTES:
        return crowded()

    rows, part = None, None
    arrived = [top_rows]
    for stage in range(n_section):
        last = stage == n_section - 1
        inputs = list(arrived) + ([place] if stage > 0 else [])
        inputs += [down, to_gate, to_up, gate, up, cols]
        if last:
            inputs += [rows, part, left, right_map, sketch]
            out = (pltpu.VMEM((n_rows, feat), BF16),)
        else:
            inputs += [comp] + ([rows, part] if stage > 0 else [])
            out = tuple(shape(share, feat) for _ in range(n_expert))
            out += (shape(n_rows, feat), shape(n_rows, feat))
        results = call(
            functools.partial(
                layer, len(arrived), 0 if last else n_expert, stage > 0, stage, n_section, n_extra
            ),
            out,
            inputs,
            scratch=[
                pltpu.VMEM((n_rows, hidden), BF16),
                pltpu.VMEM((n_rows, hidden), BF16),
                pltpu.VMEM((n_rows, feat), BF16),
            ],
            limit=16 << 20,
        )
        if last:
            back = exchange(results[0])
            break
        part, rows = results[n_expert:]
        arrived = send_down(results[:n_expert], n_section - 1 - stage, n_expert)

    def direct(*_):
        return call(
            functools.partial(finish, n_expert, block, used, n_extra, q_dev),
            (
                shape(1, n_micro, tok_dev, feat),
                shape(1, q_dev, sketch_dim * sketch_dim, dtype=F32),
            ),
            (back, slots),
        )

    return lax.cond(over[0, 0] > share, crowded, direct)


def solution(mesh):
    placed = (
        P("section", None, "expert", None),
        P(None, "expert", None),
        P("section", None, "expert", None),
        P("section", None, "expert", None),
        P(None, "expert"),
        P("section", "expert", None),
        P("section", "expert", None),
        P("section", "expert", None),
        P("section", "expert", None),
        P("section", None, None),
    )
    return jax.shard_map(
        on_device,
        mesh=mesh,
        in_specs=placed,
        out_specs=(P("section", None, "expert", None), P("section", "expert", None)),
        check_vma=False,
    )
```

```python
import functools
import math

import jax
import jax.numpy as jnp
from jax import lax
from jax.experimental import pallas as pl
from jax.experimental.pallas import tpu as pltpu
from jax.sharding import PartitionSpec as P

EXPERTS = 8
EXM = 4
CAP = 3
LANES = 128
MOST_PERMUTES = 8
NARROW = (1536, 1)
WIDEN = (2048, 1)
FORWARD = 512

F32 = jnp.float32
BF16 = jnp.bfloat16
VMEM = pl.BlockSpec(memory_space=pltpu.VMEM)
HBM = pl.BlockSpec(memory_space=pltpu.HBM)


def contract(a, b, dim_a, dim_b):
    return lax.dot_general(a, b, (((dim_a,), (dim_b,)), ((), ())), preferred_element_type=F32)


def iota(shape, dim):
    return lax.broadcasted_iota(jnp.int32, shape, dim)


def ones_where(mask):
    return jnp.where(mask, 1.0, 0.0).astype(F32)


def partner(device, turn, amount):
    if amount & (amount - 1) == 0:
        return device ^ turn
    return (turn + 2 * amount - device) % amount


def size_of(arrays):
    return sum(a.dtype.itemsize * a.size for a in arrays)


def over_tiles(size, shape, body):
    tile, together = math.gcd(size, shape[0]), shape[1]

    def step(number, carry):
        body(pl.ds(pl.multiple_of(number * tile, tile), tile))
        return carry

    if size == tile:
        body(pl.ds(0, tile))
        return
    lax.fori_loop(0, size // tile, step, 0, unroll=math.gcd(size // tile, together))


def call(kernel, out_shape, inputs, spec=VMEM, scratch=(), limit=12 << 20):
    return pl.pallas_call(
        kernel,
        out_shape=out_shape,
        in_specs=[spec] * len(inputs),
        out_specs=tuple(VMEM for _ in out_shape),
        scratch_shapes=list(scratch),
        compiler_params=pltpu.CompilerParams(vmem_limit_bytes=limit),
    )(*inputs)


def copy_all(pairs, sems):
    copies = []
    for number, (source, target) in enumerate(pairs):
        copies.append(pltpu.make_async_copy(source, target, sems.at[number]))
        copies[-1].start()
    for copy in copies:
        copy.wait()


def names(fields, top_k, group):
    hit = fields[0:1, :] == group
    for k in range(1, top_k):
        hit = hit | (fields[k : k + 1, :] == group)
    return ones_where(hit)


def prepare(n_section, n_expert, block, ids_hbm, w_hbm, ex_hbm, x_hbm, top_hbm, *refs):
    send_ref, slots_ref = refs[:2]
    ids_ref, w_ref, ex_ref, x_ref, top_ref, sems = refs[2:]
    from_hbm = (ids_hbm, w_hbm, ex_hbm, x_hbm, top_hbm)
    copy_all(list(zip(from_hbm, (ids_ref, w_ref, ex_ref, x_ref, top_ref))), sems)
    n_micro, top_k, tok_dev = ids_ref.shape[1:]
    tokens = n_micro * tok_dev
    n_all = n_expert * tokens
    n_fields = 2 * top_k + 1
    feat = x_ref.shape[3]
    section, me = lax.axis_index("section"), lax.axis_index("expert")
    padded = -(-n_fields // 8) * 8
    local = jnp.zeros((padded, tokens), F32)
    packed = jnp.zeros((padded, n_all), F32)
    for m in range(n_micro):
        row = iota((padded, tok_dev), 0)
        example = ex_ref[m : m + 1, :] + m * EXM
        fields = jnp.where(row == 2 * top_k, example.astype(F32), 0.0)
        for k in range(top_k):
            fields = jnp.where(row == k, ids_ref[0, m, k : k + 1, :].astype(F32), fields)
            fields = jnp.where(row == top_k + k, w_ref[0, m, k : k + 1, :].astype(F32), fields)
        here = iota((tok_dev, tokens), 1) == m * tok_dev + iota((tok_dev, tokens), 0)
        local = local + contract(fields, ones_where(here), 1, 0)
        there = me * tokens + m * tok_dev + iota((tok_dev, n_all), 0)
        packed = packed + contract(fields, ones_where(iota((tok_dev, n_all), 1) == there), 1, 0)
    early, late = iota((tokens, tokens), 0), iota((tokens, tokens), 1)
    before = ones_where((early // tok_dev == late // tok_dev) & (early < late))

    def slots_in(height):
        at = (n_expert * height, tokens)
        group = (iota(at, 0) // (height * (n_expert // EXPERTS))).astype(F32)
        hit = names(local, top_k, group)
        position = contract(hit, before, 1, 0)
        slot = iota(at, 0) % block - CAP * (iota(at, 1) // tok_dev)
        fits = (hit > 0.5) & (slot >= 0) & (slot < CAP) & (position == slot.astype(F32))
        return ones_where(fits)

    slots_ref[...] = slots_in(block).astype(BF16)
    both = slots_in(2 * block)
    second = iota(both.shape, 0) % (2 * block) >= block
    for_saved = jnp.where(second, 0.0, both).astype(BF16)
    for_top = jnp.where(second & (section == n_section - 1), both, 0.0).astype(BF16)
    saved = jnp.concatenate([x_ref[0, m] for m in range(n_micro)], axis=0)
    top = jnp.concatenate([top_ref[m] for m in range(n_micro)], axis=0)
    send_ref[...] = (contract(for_saved, saved, 1, 0) + contract(for_top, top, 1, 0)).astype(BF16)
    spare_at = iota((2 * n_expert * block, n_all), 0) % (2 * block)
    for number, (at_row, lanes) in enumerate(field_places(n_fields, n_all, feat, n_micro * CAP)):
        field = jnp.broadcast_to(packed[number : number + 1, :], spare_at.shape)
        kept = send_ref[:, lanes].astype(F32)
        send_ref[:, lanes] = jnp.where(spare_at == at_row, field, kept).astype(BF16)


def field_places(n_fields, n_all, feat, first_row):
    per_row = feat // n_all
    for number in range(n_fields):
        at = number % per_row * n_all
        yield first_row + number // per_row, slice(at, at + n_all)


def collect(block, used, n_fields, x_ref, fields_ref):
    n_all = fields_ref.shape[1]
    rows, feat = x_ref.shape
    total = jnp.zeros(fields_ref.shape, F32)
    for number, (at_row, lanes) in enumerate(field_places(n_fields, n_all, feat, used)):
        spare = iota((rows, n_all), 0) % (2 * block) == at_row
        kept = jnp.where(spare, x_ref[:, lanes].astype(F32), 0.0)
        field = jnp.sum(kept, axis=0, keepdims=True)
        total = jnp.where(iota(fields_ref.shape, 0) == number, field, total)
    fields_ref[...] = total


def plan(
    n_section, n_expert, n_micro, tok_dev, top_k, block, share, q_dev, *refs
):
    around, refs = refs[:n_section], refs[n_section:]
    comp_ref, place_ref, cols_ref, sketch_ref, over_ref = refs
    n_all = around[0].shape[1]
    tokens = n_micro * tok_dev
    hsplit = n_expert // EXPERTS
    rows = n_expert * block
    section, me = lax.axis_index("section"), lax.axis_index("expert")
    mine, below, above = around[0][...], around[-1][...], around[1 % n_section][...]
    group = (me // hsplit).astype(F32)
    hit = names(mine, top_k, group)
    early, late = iota((n_all, n_all), 0), iota((n_all, n_all), 1)
    before = ones_where(early < late)
    near = ones_where((early // tok_dev == late // tok_dev) & (early < late))
    lane = iota((8, n_all), 1)
    count = contract(jnp.broadcast_to(hit, (8, n_all)), near, 1, 0)
    slot = (lane // tokens) * block + (lane // tok_dev) % n_micro * CAP
    slot = (slot.astype(F32) + count)[0:1, :]
    held = ones_where((iota((rows, n_all), 0).astype(F32) == slot) & (hit > 0.5))
    weight = jnp.zeros((1, n_all), F32)
    for k in range(top_k):
        weight = weight + jnp.where(
            mine[k : k + 1, :] == group, mine[top_k + k : top_k + k + 1, :], 0.0
        )
    first = ones_where((mine[0:1, :] == group) & (me % hsplit == 0))
    column = iota((rows, LANES), 1)
    weight_col = jnp.sum(held * weight, axis=1, keepdims=True)
    first_col = jnp.sum(held * first, axis=1, keepdims=True)
    cols_ref[...] = jnp.where(column == 0, weight_col, jnp.where(column == 1, first_col, 0.0))

    held_b = held.astype(BF16)
    peers = (partner(me, iota((n_expert, n_all), 0), n_expert) // hsplit).astype(F32)
    for other, to_row in ((below, True), (above, False)):
        both = names(other, top_k, peers) * hit
        position = contract(both, before, 1, 0)
        picks = []
        for turn in range(n_expert):
            chosen = position[turn : turn + 1, :] == iota((share, n_all), 0).astype(F32)
            picks.append(ones_where(chosen) * both[turn : turn + 1, :])
        picks = jnp.concatenate(picks, axis=0).astype(BF16)
        if to_row:
            comp_ref[...] = contract(picks, held_b, 1, 1).astype(BF16)
        else:
            place_ref[...] = contract(held_b, picks, 1, 1).astype(BF16)

    place = iota((rows, n_all), 0)
    target = (place // block) * q_dev
    local = me // hsplit
    inside = (local >= target % EXPERTS) & (local < target % EXPERTS + q_dev)
    example = mine[2 * top_k : 2 * top_k + 1, :]
    fits = inside & (example == (target // EXPERTS).astype(F32))
    for part_no in range(sketch_ref.shape[0]):
        at_row = place % block == n_micro * CAP + part_no
        terms = jnp.where(fits & at_row, weight, 0.0).astype(BF16)
        sketch_ref[part_no] = contract(terms, held_b, 1, 1).astype(BF16)

    expert = iota((EXPERTS, n_all), 0).astype(F32)
    most = jnp.zeros((1, 1), F32)
    upper = names(mine, top_k, expert)
    for turn in range(1, n_section + 1):
        lower, upper = upper, names(around[turn % n_section][...], top_k, expert)
        shared = jnp.max(contract(upper, lower, 1, 1), axis=(0, 1), keepdims=True)
        wraps = (section + turn) % n_section == 0
        most = jnp.maximum(most, jnp.where(wraps, 0.0, shared))
    over_ref[...] = jnp.broadcast_to(most, over_ref.shape)


def forward(
    block, both_ref, gate_hbm, up_hbm, down_hbm, left_hbm, right_hbm,
    to_gate_ref, to_up_ref, left_ref, top_ref, gate_ref, up_ref, down_ref, right_map, left_map, sems,
):
    n_rows, hidden = to_gate_ref.shape
    feat = top_ref.shape[1]
    tile = math.gcd(hidden, FORWARD)
    pairs = [(left_hbm, left_map)]
    for number in range(hidden // tile):
        part = pl.ds(number * tile, tile)
        pairs.append((gate_hbm.at[:, part, :], gate_ref.at[:, part, :]))
        pairs.append((up_hbm.at[:, part, :], up_ref.at[:, part, :]))
    pairs += [(down_hbm, down_ref), (right_hbm, right_map)]
    copies = [pltpu.make_async_copy(a, b, sems.at[i]) for i, (a, b) in enumerate(pairs)]
    for copy in copies:
        copy.start()
    both = both_ref[...].astype(F32).reshape(n_rows // block, 2 * block, feat)
    top_ref[...] = both[:, block:].reshape(n_rows, feat).astype(BF16)
    x = both[:, :block].reshape(n_rows, feat).astype(BF16)
    copies[0].wait()
    size = left_map.shape[1]
    left = jnp.zeros((n_rows, size), F32)
    for number in range(hidden // tile):
        part = slice(number * tile, (number + 1) * tile)
        copies[2 * number + 1].wait()
        gate = contract(x, gate_ref[0, part, :], 1, 1)
        copies[2 * number + 2].wait()
        up = contract(x, up_ref[0, part, :], 1, 1)
        sigmoid = jax.nn.sigmoid(gate)
        silu = gate * sigmoid
        to_up_ref[:, part] = silu
        to_gate_ref[:, part] = up * sigmoid * (1.0 + gate * (1.0 - sigmoid))
        left = left + contract((silu * up).astype(BF16), left_map[0, :, part], 1, 1)
    left = left.astype(BF16)
    for at in range(0, left_ref.shape[1], feat):
        lane, axis = at + iota((size, feat), 1), iota((size, feat), 0)
        over_left = ones_where(axis == lane // size).astype(BF16)
        left_ref[:, at : at + feat] = contract(left, over_left, 1, 0).astype(BF16)
    for copy in copies[-2:]:
        copy.wait()


def layer(n_arrived, n_sent, n_before, stage, n_section, n_extra, *refs):
    refs = list(refs)
    take = lambda amount: [refs.pop(0) for _ in range(amount)]
    arrived = take(n_arrived)
    place = take(1)[0] if n_arrived > 1 else None
    down, to_gate, to_up, gate, up, cols = take(6)
    comp = take(1)[0] if n_sent else None
    rows_before, part_before = take(2) if n_before else (None, None)
    if not n_sent:
        left_ref, right_proj, sketch = take(3)
    sent = take(n_sent)
    part_ref, rows_ref = take(2) if n_sent else take(1) + [None]
    grad_gate, grad_up, rows_now = refs
    feat = rows_now.shape[1]
    live = lax.axis_index("section") == n_section - 1 - stage

    @pl.when(live)
    def _():
        if n_arrived > 1:
            pieces = jnp.concatenate([ref[...].astype(F32) for ref in arrived], axis=0)
            rows = contract(place[...], pieces.astype(BF16), 1, 0).astype(BF16)
        else:
            rows = arrived[0][...]
        rows_now[...] = rows
        def narrow(part):
            grad_hidden = contract(rows_now[...], down[0, part, :], 1, 1)
            grad_gate[:, part] = (grad_hidden * to_gate[:, part]).astype(BF16)
            grad_up[:, part] = (grad_hidden * to_up[:, part]).astype(BF16)

        over_tiles(grad_gate.shape[1], NARROW, narrow)

        def widen(part):
            total = contract(grad_gate[...], gate[0, :, part], 1, 0)
            total = total + contract(grad_up[...], up[0, :, part], 1, 0)
            kept = rows_now[:, part].astype(F32) * cols[:, 1:2]
            total = (total * cols[:, 0:1] + kept).astype(BF16)
            part_ref[:, part] = total
            if n_sent:
                chosen = contract(comp[...], total, 1, 0)
                share = chosen.shape[0] // n_sent
                for turn in range(n_sent):
                    sent[turn][:, part] = chosen[turn * share : (turn + 1) * share].astype(BF16)

        over_tiles(feat, WIDEN, widen)

    @pl.when(jnp.logical_not(live))
    def _():
        if n_before:
            rows_now[...] = rows_before[...]
            part_ref[...] = part_before[...]
        else:
            rows_now[...] = jnp.zeros(rows_now.shape, BF16)
            part_ref[...] = jnp.zeros(part_ref.shape, BF16)

    if n_sent:
        rows_ref[...] = rows_now[...]
        return
    right = contract(rows_now[...], right_proj[0], 1, 1)
    high = right.astype(BF16)
    low = (right - high.astype(F32)).astype(BF16)
    size = right.shape[1]
    width = math.gcd(feat, 2 * LANES)
    over_right = iota((size, width), 0) == iota((size, width), 1) % size
    over_right = ones_where(over_right).astype(BF16)
    right = contract(high, over_right, 1, 0) + contract(low, over_right, 1, 0)
    right = jnp.concatenate([right] * (feat // width), axis=1)
    for number in range(n_extra):
        part = slice(number * feat, (number + 1) * feat)
        outer = left_ref[:, part].astype(F32) * right
        terms = contract(sketch[number], outer.astype(BF16), 1, 0)
        part_ref[...] = (part_ref[...].astype(F32) + terms).astype(BF16)


def plan_and_layer(planner, layers, n_around, *refs):
    around, inputs, refs = refs[:n_around], refs[n_around : n_around + 6], refs[n_around + 6 :]
    comp, place, cols, sketch, over = refs[:5]
    planner(*around, comp, place, cols, sketch, over)
    layers(*inputs, cols, comp, *refs[5:])


def finish(n_expert, block, used, n_extra, q_dev, back_ref, slots_ref, grad_ref, sketch_ref):
    me = lax.axis_index("expert")
    hsplit = n_expert // EXPERTS
    n_micro, tok_dev, feat = grad_ref.shape[1:]
    rows = n_expert * block
    start = (me * q_dev) % EXPERTS
    group = iota((q_dev, rows), 1) // (block * hsplit)
    owner = group == start + iota((q_dev, rows), 0)
    back = back_ref[...]
    total = contract(slots_ref[...], back, 0, 0)
    for m in range(n_micro):
        grad_ref[0, m] = total[m * tok_dev : (m + 1) * tok_dev].astype(BF16)
    for number in range(n_extra):
        at_row = iota((q_dev, rows), 1) % block == used + number
        picks = ones_where(owner & at_row).astype(BF16)
        sketch_ref[0, :, number * feat : (number + 1) * feat] = contract(picks, back, 1, 0)


def send_down(blocks, section, n_expert):
    window = 5
    quick, far = [0, n_expert // 4, 1], [n_expert // 2 + 1, n_expert // 2]
    late = [turn for turn in reversed(range(n_expert)) if turn not in quick + far]
    order = quick + far + late
    arrived = [None] * n_expert
    for place, turn in enumerate(order):
        pairs = [
            (section * n_expert + e, (section - 1) * n_expert + partner(e, turn, n_expert))
            for e in range(n_expert)
        ]
        block = blocks[turn]
        if place >= window:
            earlier = order[place - window]
            block, arrived[earlier] = lax.optimization_barrier((block, arrived[earlier]))
        arrived[turn] = lax.ppermute(block, ("section", "expert"), pairs)
    return arrived


def by_owners(block, used, n_extra, q_dev, arrays, slots, x_rows, top_rows, cols, sketch):
    top_grad, gate_weight, up_weight, down_weight, left_proj, right_proj = arrays
    n_section, n_expert = lax.axis_size("section"), lax.axis_size("expert")
    section = lax.axis_index("section")
    n_micro, tok_dev, feat = top_grad.shape
    tokens = n_micro * tok_dev
    n_rows = n_expert * block

    def exchange(rows):
        blocks = rows.reshape(n_expert, block, feat)
        blocks = lax.all_to_all(blocks, "expert", split_axis=0, concat_axis=0, tiled=True)
        return blocks.reshape(n_rows, feat)

    gate, up, down = gate_weight[0], up_weight[0], down_weight[0]
    pre_gate = contract(x_rows, gate, 1, 1)
    pre_up = contract(x_rows, up, 1, 1)
    sigmoid = jax.nn.sigmoid(pre_gate)
    to_up = pre_gate * sigmoid
    to_gate = pre_up * sigmoid * (1.0 + pre_gate * (1.0 - sigmoid))
    left = contract((to_up * pre_up).astype(BF16), left_proj[0], 1, 0).astype(BF16)
    size = left.shape[1]
    rows = top_rows
    right = jnp.zeros((n_rows, size), F32)
    own = jnp.zeros((tokens, feat), BF16)
    for stage in range(n_section):
        live = section == n_section - 1 - stage
        if stage > 0:
            hop = [(n_section - stage, n_section - 1 - stage)]
            out_grad = lax.ppermute(new_grad, "section", hop)
            rows = exchange(contract(slots, out_grad, 1, 0).astype(BF16))
        grad_hidden = contract(rows, down, 1, 1)
        part = contract((grad_hidden * to_gate).astype(BF16), gate, 1, 0)
        part = part + contract((grad_hidden * to_up).astype(BF16), up, 1, 0)
        part = part * cols[:, 0:1] + rows.astype(F32) * cols[:, 1:2]
        right = right + jnp.where(live, contract(rows, right_proj[0], 1, 0), 0.0)
        back = exchange(part.astype(BF16))
        new_grad = contract(slots, back, 0, 0).astype(BF16)
        own = jnp.where(live, new_grad, own)
    outer = (left.astype(F32)[:, :, None] * right[:, None, :]).astype(BF16)
    outer = outer.reshape(n_rows, n_extra * feat)
    terms = jnp.zeros((n_rows, feat), F32)
    for number in range(n_extra):
        here = outer[:, number * feat : (number + 1) * feat]
        terms = terms + contract(sketch[number], here, 1, 0)
    back = exchange(terms.astype(BF16)).reshape(EXPERTS, n_expert // EXPERTS, block, feat)
    back = back[:, :, used : used + n_extra].astype(F32).sum(axis=1)
    back = back.reshape(EXPERTS, n_extra * feat)
    start = (lax.axis_index("expert") * q_dev) % EXPERTS
    found = lax.dynamic_slice_in_dim(back, start, q_dev, 0)
    return own.reshape(1, n_micro, tok_dev, feat), found[None]


def on_device(
    saved_inputs,
    top_grad,
    expert_ids,
    route_weights,
    example_ids,
    gate_weight,
    up_weight,
    down_weight,
    left_proj,
    right_proj,
):
    n_section = lax.axis_size("section")
    n_expert = lax.axis_size("expert")
    n_micro, tok_dev, feat = saved_inputs.shape[1:]
    top_k = expert_ids.shape[3]
    hidden = gate_weight.shape[1]
    tokens = n_micro * tok_dev
    sketch_dim = left_proj.shape[2]
    used = n_micro * CAP
    n_extra = sketch_dim * sketch_dim // feat
    block = -(-(used + n_extra) // 8) * 8
    n_rows = n_expert * block
    q_dev = n_micro * EXM * EXPERTS // n_expert
    share = -(-(n_expert * used // 2) // 8) * 8
    n_picks = n_expert * share

    def shape(*dims, dtype=BF16):
        return jax.ShapeDtypeStruct(dims, dtype)

    arrays = (
        expert_ids.transpose(0, 1, 3, 2),
        route_weights.transpose(0, 1, 3, 2),
        example_ids,
        saved_inputs,
        top_grad,
    )
    send, slots = call(
        functools.partial(prepare, n_section, n_expert, block),
        (pltpu.VMEM((2 * n_rows, feat), BF16), shape(n_rows, tokens)),
        arrays,
        HBM,
        [pltpu.VMEM(a.shape, a.dtype) for a in arrays] + [pltpu.SemaphoreType.DMA((5,))],
        58 << 20,
    )

    def exchange(rows):
        blocks = rows.reshape(n_expert, rows.shape[0] // n_expert, feat)
        blocks = lax.all_to_all(blocks, "expert", split_axis=0, concat_axis=0, tiled=True)
        return blocks.reshape(rows.shape)

    both = exchange(send)
    (fields,) = call(
        functools.partial(collect, block, used, 2 * top_k + 1),
        (shape(-(-(2 * top_k + 1) // 8) * 8, n_expert * tokens, dtype=F32),),
        (both,),
    )
    around = [fields]
    for turn in range(1, n_section):
        pairs = [(i, (i - turn) % n_section) for i in range(n_section)]
        around.append(lax.ppermute(fields, "section", pairs))
    tile = math.gcd(hidden, FORWARD)
    left_map, right_map = left_proj.transpose(0, 2, 1), right_proj.transpose(0, 2, 1)
    stored = (gate_weight, up_weight, down_weight, left_map, right_map)
    to_gate, to_up, left, top_rows, gate, up, down, right_map = pl.pallas_call(
        functools.partial(forward, block),
        out_shape=(
            pltpu.VMEM((n_rows, hidden), F32),
            pltpu.VMEM((n_rows, hidden), F32),
            pltpu.VMEM((n_rows, n_extra * feat), BF16),
            shape(n_rows, feat),
        )
        + tuple(pltpu.VMEM(stored[i].shape, BF16) for i in (0, 1, 2, 4)),
        in_specs=[VMEM] + [HBM] * len(stored),
        out_specs=(VMEM,) * 8,
        scratch_shapes=[
            pltpu.VMEM(left_map.shape, BF16),
            pltpu.SemaphoreType.DMA((3 + 2 * (hidden // tile),)),
        ],
        compiler_params=pltpu.CompilerParams(vmem_limit_bytes=38 << 20),
    )(both, *stored)
    raw = (top_grad, gate_weight, up_weight, down_weight, left_proj, right_proj)

    def crowded(*_):
        x_rows = both.reshape(n_expert, 2 * block, feat)[:, :block].reshape(n_rows, feat)
        return by_owners(
            block, used, n_extra, q_dev, raw, slots, x_rows, top_rows, cols, sketch
        )

    planner = functools.partial(
        plan, n_section, n_expert, n_micro, tok_dev, top_k, block, share, q_dev
    )
    plan_out = (
        shape(n_picks, n_rows),
        shape(n_rows, n_picks),
        shape(n_rows, LANES, dtype=F32),
        shape(n_extra, n_rows, n_rows),
        shape(8, LANES, dtype=F32),
    )
    if n_expert > MOST_PERMUTES:
        limit = (12 << 20) + 16 * n_rows * n_picks
        _, _, cols, sketch, _ = call(planner, plan_out, around, limit=limit)
        return crowded()

    rows, part = None, None
    arrived = [top_rows]
    for stage in range(n_section):
        last = stage == n_section - 1
        inputs = list(arrived) + ([place] if stage > 0 else [])
        inputs += [down, to_gate, to_up, gate, up] + ([cols] if stage else [])
        if last:
            inputs += [rows, part, left, right_map, sketch]
            out = (pltpu.VMEM((n_rows, feat), BF16),)
        else:
            inputs += [comp, rows, part] if stage else []
            out = tuple(shape(share, feat) for _ in range(n_expert))
            out += (shape(n_rows, feat), shape(n_rows, feat))
        kernel = functools.partial(
            layer, len(arrived), 0 if last else n_expert, stage > 0, stage, n_section, n_extra
        )
        if not stage:
            kernel = functools.partial(plan_and_layer, planner, kernel, n_section)
            inputs = [*around, *arrived, down, to_gate, to_up, gate, up]
            out = plan_out + out
        results = call(
            kernel,
            out,
            inputs,
            scratch=[
                pltpu.VMEM((n_rows, hidden), BF16),
                pltpu.VMEM((n_rows, hidden), BF16),
                pltpu.VMEM((n_rows, feat), BF16),
            ],
            limit=16 << 20,
        )
        if not stage:
            comp, place, cols, sketch, over = results[:5]
            results = results[5:]
        if last:
            back = exchange(results[0])
            break
        part, rows = results[n_expert:]
        arrived = send_down(results[:n_expert], n_section - 1 - stage, n_expert)

    def direct(*_):
        return call(
            functools.partial(finish, n_expert, block, used, n_extra, q_dev),
            (
                shape(1, n_micro, tok_dev, feat),
                shape(1, q_dev, sketch_dim * sketch_dim, dtype=F32),
            ),
            (back, slots),
        )

    return lax.cond(over[0, 0] > share, crowded, direct)


def solution(mesh):
    placed = (
        P("section", None, "expert", None),
        P(None, "expert", None),
        P("section", None, "expert", None),
        P("section", None, "expert", None),
        P(None, "expert"),
        P("section", "expert", None),
        P("section", "expert", None),
        P("section", "expert", None),
        P("section", "expert", None),
        P("section", None, None),
    )
    return jax.shard_map(
        on_device,
        mesh=mesh,
        in_specs=placed,
        out_specs=(P("section", None, "expert", None), P("section", "expert", None)),
        check_vma=False,
    )
```
